128 devices in a mesh: dp: 32 (over x, y, core), tensor: 4 (over z).
Axes of the slice: x: 4, y: 4, z: 4, core: 2. Of those that a mesh axis runs over, the one named last changes fastest.
Arguments:
- partial_grads: bfloat16 [32, 24, 1024, 1024], P('dp', 'tensor'), may hold values from -5 to 5
- owner_slots: int32 [24, 2], replicated, may hold values from 0 to 127, as said below
- statistics: float32 [32, 4, 1, 1024, 1024], P('dp', 'tensor'), may hold values from -6 to 6
- inv_roots: bfloat16 [32, 4, 1, 1024, 1024], P('dp', 'tensor'), may hold values from -0.1875 to 0.1875
Outputs:
- new_stats: float32 [32, 4, 1, 1024, 1024], P('dp', 'tensor')
- update: bfloat16 [24, 1024, 1024], P('tensor', 'dp')
The draws below stay inside these ranges and needn't reach their ends.
Inputs may be any that keep to these rules, and one draw needn't show every extreme that they name: `owner_slots`: the 48 entries name distinct slots; some device has all 1 of its slots named.
All inputs are finite; a program needn't handle non-finite values.
Results may differ from the reference program's by a relative error of at most 0.024.
Values may be sent and summed in bfloat16 or wider, within the bound.
A program may use at most 128 MiB of HBM per device.

```python
import jax
import jax.numpy as jnp
from jax import lax

B = 1024
NB = 24
CAP = 1
N_DP = 32
N_TENSOR = 4


def draw_owner_slots(key, part):
    key = jax.random.fold_in(key, 11)
    key_devices, key_sides = jax.random.split(key)
    device_count = N_DP * N_TENSOR
    shuffled = jax.random.permutation(key_devices, device_count).astype(jnp.int32)
    position = jnp.arange(2 * NB, dtype=jnp.int32)
    slot_ids = shuffled[position // CAP] * CAP + position % CAP
    side_order = jax.random.permutation(key_sides, 2 * NB).astype(jnp.int32)
    owner_table = jnp.zeros((2 * NB,), jnp.int32).at[side_order].set(slot_ids)
    return owner_table.reshape(NB, 2)


def spiked(entries, stream_key, source, target, blocks, factor):
    owner, partner = [(jnp.arange(entries.shape[axis_at]) // (entries.shape[axis_at] // blocks)).reshape([-1 if axis == axis_at else 1 for axis in range(entries.ndim)]) for axis_at in (source, target)]
    chosen = jax.random.permutation(stream_key, blocks)[partner]
    strong = (owner == chosen) | (owner == (partner + blocks // 2) % blocks)
    return jnp.where(strong, factor * entries, entries)


def block_scale(stream_key, shape, shards, least, high):
    level = 1.0
    for dim, blocks in shards:
        heights = jax.random.uniform(jax.random.fold_in(jax.random.fold_in(stream_key, 6), dim), (blocks,), jnp.float32, least / len(shards), high / len(shards))
        level = level * jnp.repeat(jnp.exp(heights), shape[dim] // blocks).reshape((-1,) + (1,) * (len(shape) - 1 - dim))
    return level


def bell_draw(key, dims, scale, bound, cuts=(), kind=jnp.bfloat16):
    entries = scale * jax.random.normal(key, dims, jnp.float32)
    if cuts:
        entries = entries * block_scale(key, dims, cuts, -0.22, 0.18)
    return jnp.clip(entries, -bound, bound).astype(kind)


def gaussian_with(stream_key, extent, spread, reach, shards, heavy, kind=jnp.bfloat16):
    array = spread * jax.random.normal(stream_key, extent, jnp.float32)
    if shards:
        array = array * block_scale(stream_key, extent, shards, -0.22, 0.18)
    return jnp.clip(spiked(array, jax.random.fold_in(stream_key, 3), *heavy), -reach, reach).astype(kind)


def setup_inputs(seed: int = 0) -> dict:
    seeds = jax.random.split(jax.random.key(seed), 5)
    return {
        "partial_grads": gaussian_with(seeds[0], (N_DP, NB, B, B), (1.0 / N_DP ** 0.5), 5.0, ((0, 32), (1, 4)), (0, 2, 32, 2.75)),
        "owner_slots": draw_owner_slots(jax.random.fold_in(seeds[4], 71), 0),
        "statistics": bell_draw(seeds[2], (N_DP, N_TENSOR, CAP, B, B), 1.0, 6.0, ((0, 32), (1, 4)), jnp.float32),
        "inv_roots": bell_draw(seeds[3], (N_DP, N_TENSOR, CAP, B, B), B ** -0.5, 0.1875, ((0, 32), (1, 4))),
    }


decay_rate = 0.9


def reference(partial_grads, owner_slots, statistics, inv_roots):
    slot_count = N_DP * N_TENSOR * CAP
    old_stats = statistics.reshape(slot_count, B, B)
    slot_roots = inv_roots.reshape(slot_count, B, B)
    gram_scale = B ** -0.5

    def visit_block(running, block_index):
        replicas = lax.dynamic_index_in_dim(partial_grads, block_index, 1, False)
        block_grad = jnp.sum(replicas.astype(jnp.float32), axis=0).astype(jnp.bfloat16)
        left_slot = owner_slots[block_index, 0]
        right_slot = owner_slots[block_index, 1]
        left_gram = jnp.dot(block_grad, block_grad.T, preferred_element_type=jnp.float32) * gram_scale
        right_gram = jnp.dot(block_grad.T, block_grad, preferred_element_type=jnp.float32) * gram_scale
        running = running.at[left_slot].set(decay_rate * old_stats[left_slot] + (1 - decay_rate) * left_gram)
        running = running.at[right_slot].set(decay_rate * old_stats[right_slot] + (1 - decay_rate) * right_gram)
        mixed = jnp.dot(slot_roots[left_slot], block_grad, preferred_element_type=jnp.float32).astype(jnp.bfloat16)
        result = jnp.dot(mixed, slot_roots[right_slot], preferred_element_type=jnp.float32).astype(jnp.bfloat16)
        return running, result

    new_stats, update = lax.scan(visit_block, old_stats, jnp.arange(NB, dtype=jnp.int32))
    return new_stats.reshape(statistics.shape), update
```

```python
import functools

import jax
import jax.numpy as jnp
from jax import lax
from jax.experimental import pallas as pl
from jax.experimental.pallas import tpu as pltpu
from jax.sharding import PartitionSpec as P

decay_rate = 0.9
MESH = pl.DeviceIdType.MESH
f32 = jnp.float32
bf16 = jnp.bfloat16
lo, hi = pl.ds(0, 3), pl.ds(3, 3)


def place():
    d = lax.axis_index("dp")
    return lax.div(d, 8), lax.rem(lax.div(d, 2), 4), lax.rem(d, 2), lax.axis_index("tensor")


def wrap(v):
    return lax.rem(v + 8, 4)


def remote(src, dst, send, recv, device):
    return pltpu.make_async_remote_copy(
        src_ref=src, dst_ref=dst, send_sem=send, recv_sem=recv, device_id=device, device_id_type=MESH
    )


class Net:
    def __init__(self, send, recv):
        self.x, self.y, self.c, self.t = place()
        self.send, self.recv, self.count, self.open = send, recv, 0, []
        self.at = {"x": self.x, "y": self.y, "z": self.t}
        self.pair = ((self.x * 4 + self.y) * 2 + 1 - self.c, self.t)

    def near(self, axis, step, swap=0):
        x, y, t = [wrap(self.at[a] + step) if a == axis else self.at[a] for a in "xyz"]
        return ((x * 4 + y) * 2 + (1 - self.c if swap else self.c), t)

    def greet(self):
        barrier = pltpu.get_barrier_semaphore()
        peers = [self.pair] + [self.near(axis, step) for axis in "xyz" for step in (1, -1)]
        peers += [self.near(axis, step, 1) for axis in "xy" for step in (1, -1)]
        for peer in peers:
            pl.semaphore_signal(barrier, inc=1, device_id=peer, device_id_type=MESH)
        pl.semaphore_wait(barrier, len(peers))

    def make(self, src, dst, device):
        copy = remote(src, dst, self.send.at[self.count], self.recv.at[self.count], device)
        self.count += 1
        return copy

    def start(self, src, dst, device, when=None):
        copy = self.make(src, dst, device)
        if when is None:
            copy.start()
        else:
            pl.when(when)(copy.start)
        self.open.append((copy, when))
        return copy

    def local(self, src, dst):
        copy = pltpu.make_async_copy(src, dst, self.send.at[self.count])
        self.count += 1
        copy.start()
        return copy

    def close(self):
        for copy, when in self.open:
            if when is None:
                copy.wait_send()
            else:
                pl.when(when)(copy.wait_send)


class Exchange:
    def __init__(self, net, axis, src, dst, relay):
        self.net, self.axis, self.dst, self.relay = net, axis, dst, relay
        here = net.at[axis]
        self.i = [wrap(here + o) for o in range(4)]
        right, left = net.near(axis, 1), net.near(axis, -1)
        self.far = [
            net.start(src(self.i[2], 0), relay.at[0], right),
            net.start(src(self.i[2], 1), relay.at[1], left),
        ]
        self.own = net.local(src(self.i[0], None), dst(self.i[0], None))
        self.direct = [
            net.start(src(self.i[1], None), dst(self.i[0], None), right),
            net.start(src(self.i[3], None), dst(self.i[0], None), left),
        ]

        self.passed = []

    def forward(self, way):
        self.far[way].wait_recv()
        source = self.i[3 if way == 0 else 1]
        self.passed.append(
            self.net.start(self.relay.at[way], self.dst(source, way), self.net.near(self.axis, 1 - 2 * way))
        )

    def finish(self):
        self.own.wait()
        for copy in self.direct + self.passed:
            copy.wait_recv()


def half(h):
    return slice(None) if h is None else pl.ds(2 * h, 2)


class LastLeg:
    def __init__(self, net, axis, src, dst, relay):
        self.net, self.axis, self.dst, self.relay = net, axis, dst, relay
        here = net.at[axis]
        self.i = [wrap(here + o) for o in range(4)]
        self.cores = [net.c, 1 - net.c]
        every = slice(None)
        self.far = [
            net.start(src(self.i[2], way, every), relay.at[way], net.near(axis, 1 - 2 * way)) for way in range(2)
        ]
        self.arrive = [
            net.start(src(self.i[o], None, self.cores[k]), dst(self.i[0], None), net.near(axis, step, k))
            for o, step in ((1, 1), (3, -1))
            for k in range(2)
        ]
        self.own = net.local(src(self.i[0], None, self.cores[0]), dst(self.i[0], None))
        self.arrive.append(net.start(src(self.i[0], None, self.cores[1]), dst(self.i[0], None), net.pair))

    def forward(self, way):
        net = self.net
        source = self.i[3 if way == 0 else 1]
        self.far[way].wait_recv()
        self.arrive += [
            net.start(
                self.relay.at[way, :, self.cores[k]], self.dst(source, way), net.near(self.axis, 1 - 2 * way, k)
            )
            for k in range(2)
        ]

    def finish(self):
        self.own.wait()
        for copy in self.arrive:
            copy.wait_recv()


class PlaneExchange:
    def __init__(self, net, parcels, middle, landing, relay):
        self.net, self.parcels, self.middle, self.landing, self.relay = net, parcels, middle, landing, relay
        self.legs = {}

    def first(self, s):
        a, d = self.parcels, self.middle

        def parcels(i, h):
            return a(0, i, half(h)) if s == 0 else a(1, half(h), i)

        self.legs[0, s] = Exchange(
            self.net, "xy"[s], parcels, lambda i, h: d.at[s, i, half(h)], self.relay.at[0, s]
        )

    def second(self, s):
        d, z, c = self.middle, self.landing, self.net.c
        self.legs[0, s].finish()

        def land(j, h):
            return z.at[half(h), j, c, 0] if s == 0 else z.at[j, half(h), c, 1]

        self.legs[1, s] = LastLeg(
            self.net, "yx"[s], lambda j, h, k: d.at[s, half(h), j, k], land, self.relay.at[1, s]
        )

    def finish(self):
        for s in range(2):
            self.legs[1, s].finish()


class WorkerLeg:
    def __init__(self, net, s, source, target, relay):
        self.net, self.s, self.axis = net, s, "xy"[s]
        here = net.at[self.axis]
        self.target, self.relay = target, relay
        self.i = i = [wrap(here + o) for o in range(4)]
        self.two = [v < 2 if s == 0 else v >= 2 for v in i]
        wide = relay.shape[-1]
        self.cols = [pl.ds(0, wide), pl.ds(wide, wide)]

        def when(o, rank):
            return self.two[o] if rank else None

        self.when = when
        self.far = [
            [
                net.start(
                    source.at[i[2], :, rank, :, self.cols[way]],
                    relay.at[way, :, rank],
                    net.near(self.axis, 1 - 2 * way),
                    when(2, rank),
                )
                for way in range(2)
            ]
            for rank in range(2)
        ]
        self.direct = [
            [
                net.start(
                    source.at[i[o], :, rank], target.at[:, i[0], rank], net.near(self.axis, step), when(o, rank)
                )
                for o, step in ((1, 1), (3, -1))
            ]
            for rank in range(2)
        ]
        self.own = net.local(source.at[i[0]], target.at[:, i[0]])
        self.passed = [[], []]

    def forward(self, way):
        o, goal = ((3, 1), (1, 3))[way]
        for rank in range(2):
            arrived = self.far[rank][way]
            when = self.when(goal, rank)
            if when is None:
                arrived.wait_recv()
            else:
                pl.when(when)(arrived.wait_recv)
            self.passed[rank].append(
                self.net.start(
                    self.relay.at[way, :, rank],
                    self.target.at[:, self.i[o], rank, :, self.cols[way]],
                    self.net.near(self.axis, 1 - 2 * way),
                    when,
                )
            )

    def finish(self):
        self.own.wait()
        for copy in self.direct[0] + self.passed[0]:
            copy.wait_recv()

        @pl.when(self.two[0])
        def _():
            for copy in self.direct[1] + self.passed[1]:
                copy.wait_recv()


class HomeLeg:
    def __init__(self, net, s, back, home, relay):
        self.net, self.axis, self.home, self.relay = net, "xy"[s], home, relay
        here = net.at[self.axis]
        self.i = i = [wrap(here + o) for o in range(4)]
        self.two = [v < 2 if s == 0 else v >= 2 for v in i]
        wide = relay.shape[-1]
        self.cols = [pl.ds(0, wide), pl.ds(wide, wide)]
        self.far = [
            [
                net.start(
                    back.at[rank, i[2], :, self.cols[way]],
                    relay.at[way, rank],
                    net.near(self.axis, 1 - 2 * way),
                    self.when(0, rank),
                )
                for way in range(2)
            ]
            for rank in range(2)
        ]
        self.direct = [
            [
                net.start(back.at[rank, i[o]], home.at[i[0], rank], net.near(self.axis, step), self.when(0, rank))
                for o, step in ((1, 1), (3, -1))
            ]
            for rank in range(2)
        ]
        self.own = net.local(back.at[:, i[0]], home.at[i[0]])
        self.passed = [[], []]

    def when(self, o, rank):
        return self.two[o] if rank else None

    def arrived(self, copy, o, rank):
        if rank:
            pl.when(self.two[o])(copy.wait_recv)
        else:
            copy.wait_recv()

    def forward(self, way):
        o = (3, 1)[way]
        for rank in range(2):
            self.arrived(self.far[rank][way], o, rank)
            self.passed[rank].append(
                self.net.start(
                    self.relay.at[way, rank],
                    self.home.at[self.i[o], rank, :, self.cols[way]],
                    self.net.near(self.axis, 1 - 2 * way),
                    self.when(o, rank),
                )
            )

    def finish(self):
        self.own.wait()
        for rank in range(2):
            for copy, o in zip(self.direct[rank] + self.passed[rank], (3, 1, 2, 2)):
                self.arrived(copy, o, rank)


def spot(s, block):
    if block < 4:
        return block, 0
    return (block - 4, 1) if s == 0 else (block - 2, 1)


class Workers:
    def __init__(self, net):
        self.net = net
        self.is_worker = lax.rem(net.x - net.y + 4, 2) == 0
        self.is_other = lax.rem(net.x - net.y + 4, 2) == 1
        self.ij = [(net.x, net.y), (net.y, net.x)]
        self.axes = ["y", "x"]

    def rank(self, s, step):
        i, j = self.ij[s]
        return lax.div(wrap(j + step - i), 2)

    def beside(self, s):
        return self.net.near(self.axes[s], 1), self.net.near(self.axes[s], -1)


class Gather:
    def __init__(self, w, s, unit, land, relay):
        self.w, net = w, w.net
        right, left = w.beside(s)
        j = [wrap(w.ij[s][1] + o) for o in range(4)]
        self.far = [
            net.make(unit(w.rank(s, 2), 0), relay.at[0], right),
            net.make(unit(w.rank(s, 2), 1), relay.at[1], left),
        ]
        self.direct = [
            net.make(unit(w.rank(s, 1), None), land(j[0], None), right),
            net.make(unit(w.rank(s, 3), None), land(j[0], None), left),
        ]
        self.passed = [
            net.make(relay.at[0], land(j[3], 0), right),
            net.make(relay.at[1], land(j[1], 1), left),
        ]
        self.own = pltpu.make_async_copy(unit(w.rank(s, 0), None), land(j[0], None), net.send.at[net.count])
        net.count += 1

        @pl.when(w.is_worker)
        def _():
            for copy in self.far + [self.own]:
                copy.start()

        @pl.when(w.is_other)
        def _():
            for copy in self.direct:
                copy.start()

        net.open += [(copy, w.is_worker) for copy in self.far]
        net.open += [(copy, w.is_other) for copy in self.direct + self.passed]

    def forward(self):
        @pl.when(self.w.is_other)
        def _():
            for arrived, onward in zip(self.far, self.passed):
                arrived.wait_recv()
                onward.start()

    def wait_here(self):
        self.own.wait()
        for copy in self.direct + self.passed:
            copy.wait_recv()


class Spread:
    def __init__(self, w, s, unit, land, relay):
        self.w, net = w, w.net
        right, left = w.beside(s)
        j = [wrap(w.ij[s][1] + o) for o in range(4)]
        mine = w.rank(s, 0)
        self.far = [net.make(unit(j[2], 0), relay.at[0], right), net.make(unit(j[2], 1), relay.at[1], left)]
        self.direct = [
            net.make(unit(j[1], None), land(mine, None), right),
            net.make(unit(j[3], None), land(mine, None), left),
        ]
        self.passed = [
            net.make(relay.at[0], land(w.rank(s, 3), 0), right),
            net.make(relay.at[1], land(w.rank(s, 1), 1), left),
        ]
        self.own = pltpu.make_async_copy(unit(j[0], None), land(mine, None), net.send.at[net.count])
        net.count += 1

        @pl.when(w.is_worker)
        def _():
            for copy in self.far + self.direct + [self.own]:
                copy.start()

        net.open += [(copy, w.is_worker) for copy in self.far + self.direct]
        net.open += [(copy, w.is_other) for copy in self.passed]

    def forward(self):
        @pl.when(self.w.is_other)
        def _():
            for arrived, onward in zip(self.far, self.passed):
                arrived.wait_recv()
                onward.start()

    def finish(self):
        @pl.when(self.w.is_other)
        def _():
            for copy in self.direct:
                copy.wait_recv()

        @pl.when(self.w.is_worker)
        def _():
            self.own.wait()
            for copy in self.passed:
                copy.wait_recv()


class ReduceScatter:
    def __init__(self, net, parts, v):
        self.net, self.parts, self.v = net, parts, v
        at = [(net.x, net.y), (net.y, net.x)]
        self.i = [[wrap(at[s][0] + o) for o in range(4)] for s in range(2)]
        self.j = [[wrap(at[s][1] + o) for o in range(4)] for s in range(2)]
        self.loads, self.swaps, self.copies = {}, {}, {}

    def fetch(self, order):
        net, own, cin = self.net, self.v["own"], self.v["cin"]

        def view(s, i, core):
            return self.parts.at[:, i, :, core, 0] if s == 0 else self.parts.at[:, :, i, core, 1]

        for o in order:
            for s in range(2):
                i = self.i[s][o]
                self.swaps[s, o] = net.start(view(s, i, 1 - net.c), cin.at[s, i], net.pair)
                self.loads[s, o] = net.local(view(s, i, net.c), own.at[s, i])

    def ship(self, stage, s, way, src, dst):
        axis = "xy"[s] if stage < 3 else "yx"[s]
        self.copies[stage, s, way] = self.net.start(src, dst, self.net.near(axis, 1 - 2 * way))

    def ready(self, s, o):
        self.loads[s, o].wait()
        self.swaps[s, o].wait_recv()

    def add(self, out, terms, blocks):
        @pl.loop(0, blocks)
        def _(b):
            for j in range(4):
                total = terms[0][b, j].astype(f32)
                for term in terms[1:]:
                    total = total + term[b, j].astype(f32)
                out[b, j] = total.astype(bf16)

    def far(self, s):
        own, cin, first_in = self.v["own"], self.v["cin"], self.v["first_in"]
        i = self.i[s][2]
        self.ready(s, 2)
        self.add(own.at[s, i], [own.at[s, i], cin.at[s, i]], 6)
        self.ship(0, s, 0, own.at[s, i, lo], first_in.at[0, s, 0])
        self.ship(0, s, 1, own.at[s, i, hi], first_in.at[0, s, 1])

    def plain(self, way, s):
        own, cin, first_in = self.v["own"], self.v["cin"], self.v["first_in"]
        o, part = ((1, hi), (3, lo))[way]
        i = self.i[s][o]
        self.ready(s, o)
        self.add(own.at[s, i, part], [own.at[s, i, part], cin.at[s, i, part]], 3)
        self.ship(1, s, way, own.at[s, i, part], first_in.at[1, s, way])

    def merged(self, way, s):
        own, cin, first_in = self.v["own"], self.v["cin"], self.v["first_in"]
        o, part = ((1, lo), (3, hi))[way]
        i = self.i[s][o]
        self.copies[0, s, way].wait_recv()
        terms = [own.at[s, i, part], cin.at[s, i, part], first_in.at[0, s, way]]
        self.add(own.at[s, i, part], terms, 3)
        self.ship(2, s, way, own.at[s, i, part], first_in.at[2, s, way])

    def first_sum(self, s, j, b):
        own, cin, first_in = self.v["own"], self.v["cin"], self.v["first_in"]
        i = self.i[s][0]
        total = own[s, i, b, j].astype(f32) + cin[s, i, b, j].astype(f32)
        k, low = (b, 0) if b < 3 else (b - 3, 1)
        for stage, way in ((2, low), (1, 1 - low)):
            total = total + first_in[stage, s, way, k, j].astype(f32)
        return total

    def second(self, s):
        f, second_in = self.v["f"], self.v["second_in"]
        self.ready(s, 0)
        for stage in (1, 2):
            for way in range(2):
                self.copies[stage, s, way].wait_recv()
        j = self.j[s][2]
        for b in range(6):
            f[s, j, b] = self.first_sum(s, j, b).astype(bf16)
        self.ship(3, s, 0, f.at[s, j, lo], second_in.at[0, s, 0])
        self.ship(3, s, 1, f.at[s, j, hi], second_in.at[0, s, 1])

    def second_plain(self, way, s):
        f, second_in = self.v["f"], self.v["second_in"]
        o, part = ((1, hi), (3, lo))[way]
        j = self.j[s][o]
        for b in range(6):
            f[s, j, b] = self.first_sum(s, j, b).astype(bf16)
        self.ship(4, s, way, f.at[s, j, part], second_in.at[1, s, way])

    def second_merged(self, way, s):
        f, second_in = self.v["f"], self.v["second_in"]
        o, part, start = ((1, lo, 0), (3, hi, 3))[way]
        j = self.j[s][o]
        self.copies[3, s, way].wait_recv()
        for k in range(3):
            total = f[s, j, start + k].astype(f32) + second_in[0, s, way, k].astype(f32)
            f[s, j, start + k] = total.astype(bf16)
        self.ship(5, s, way, f.at[s, j, part], second_in.at[2, s, way])

    def finish(self, s, out):
        second_in = self.v["second_in"]
        for stage in (4, 5):
            for way in range(2):
                self.copies[stage, s, way].wait_recv()
        j = self.j[s][0]
        for b in range(6):
            total = self.first_sum(s, j, b)
            k, low = (b, 0) if b < 3 else (b - 3, 1)
            total = total + second_in[2, s, low, k].astype(f32)
            total = total + second_in[1, s, 1 - low, k].astype(f32)
            out[b, s] = total.astype(bf16)


(
    BLK, FAR, FETCH, G, GG, GGF, GL, GLF, MERGED, MMA, MMB, OW1, OW1F, OW2, OW2F, OWE, PLAIN, RG, RGF, RL, RLF,
    RO1, RO1F, RO2, RO2F, SEC, SECM, SECP, SH0, SH1, SP, SPF, UL, ULE, ULF, ZAF, ZF, ZM, ZP, ZSEL,
) = range(40)
ORDER = (
    (RO1, 1), (RO1, 0), (BLK,), (RO1F, 1, 1), (RO1F, 0, 1), (RO1F, 1, 0), (RO1F, 0, 0), (FETCH,), (RO2, 1),
    (RO2, 0), (RO2F, 0, 0), (RO2F, 1, 1), (RO2F, 1, 0), (FAR, 0), (PLAIN, 0, 0), (RO2F, 0, 1), (FAR, 1), (ZF,),
    (PLAIN, 1, 0), (PLAIN, 0, 1), (PLAIN, 1, 1), (ZP,), (ZM, 1), (MERGED, 0, 1), (MERGED, 1, 0),
    (MERGED, 0, 0), (MERGED, 1, 1), (ZM, 0), (SEC, 0), (SEC, 1), (SECP, 1, 1), (SECP, 0, 0), (SECP, 1, 0),
    (SECP, 0, 1), (ZSEL,), (SECM, 0, 0), (SECM, 1, 0), (SECM, 1, 1), (SECM, 0, 1), (RL, 1), (RL, 0), (G, 0),
    (G, 1), (GL, 0), (RLF, 1, 1), (GL, 1), (RLF, 1, 0), (GLF, 1, 0), (GLF, 0, 0), (RLF, 0, 0), (GLF, 0, 1),
    (GLF, 1, 1), (RLF, 0, 1), (RG, 1), (GG, 0), (GGF, 0), (ZAF, 0, 0), (ZAF, 0, 1), (ZAF, 1, 1), (RG, 0),
    (GG, 1), (GGF, 1), (ZAF, 1, 0), (RGF, 1), (OW1, 0), (RGF, 0), (OW1, 1), (SH0,), (SH1,), (MMA,),
    (OW1F, 0, 0), (OW1F, 0, 1), (OW1F, 1, 0), (OW1F, 1, 1), (MMB,), (SP,), (SPF, 0), (SPF, 1), (OW2, 1),
    (OW2, 0), (UL, 0), (OW2F, 1, 0), (UL, 1), (ULF, 0, 1), (ULF, 1, 0), (ULF, 0, 0), (OW2F, 0, 0), (ULF, 1, 1),
    (OW2F, 1, 1), (OW2F, 0, 1), (ULE,), (OWE,),
)


def step_kernel(names, *refs):
    v = dict(zip(names, refs))
    net = Net(v["send"], v["recv"])
    t, c = net.t, net.c
    owners, g, root, blocks = v["owners"], v["g"], v["root"], v["blocks"]
    every = [v["every_0"], v["every_1"]]
    net.greet()
    right, left = net.near("z", 1), net.near("z", -1)
    plane = [wrap(t + o) for o in range(4)]
    sums = ReduceScatter(net, v["parts"], v)
    workers = Workers(net)
    steps, kept = {}, {}

    def step(name):
        def keep(function):
            steps[name] = function

        return keep

    @step((FETCH,))
    def _():
        sums.fetch((2, 1, 3, 0))

    @step((BLK,))
    def _():
        @pl.loop(0, 32)
        def _(d):
            slot, block = d * 4 + t, jnp.int32(0)
            for b in range(24):
                hit = jnp.logical_or(owners[0, b] == slot, owners[1, b] == slot)
                block = jnp.where(hit, b, block)
            blocks[d] = block

    roots = PlaneExchange(
        net, lambda s, x, y: root.at[x, y, :, s], v["root_middle"], v["roots"], v["root_relay"]
    )
    parcels = v["owned_parcels"]
    owned = PlaneExchange(
        net, lambda s, x, y: parcels.at[s, x, y], v["owned_middle"], v["owned"], v["owned_relay"]
    )

    def pack_owned(s):
        kept["g_own", s].wait()
        for way in range(2):
            kept["g_pass", s, way].wait_recv()

        @pl.loop(0, 16)
        def _(chip):
            x, y = lax.div(chip, 4), lax.rem(chip, 4)
            for core in range(2):
                block = blocks[2 * chip + core]
                parcels[s, x, y, core] = every[s][lax.div(block, 6), lax.rem(block, 6)]

        owned.first(s)

    pieces, hold = v["roots"], v["hold"]
    far_in, plain_in, merged_in = v["z_far"], v["z_plain"], v["z_merged"]
    first_k, last_k = pl.ds(0, 6), pl.ds(6, 6)

    def wanted(target, k):
        slot = owners[lax.div(k, 6), target * 6 + lax.rem(k, 6)]
        d = lax.div(slot, 4)
        return lax.rem(slot, 4), pieces[lax.div(d, 8), lax.rem(lax.div(d, 2), 4), lax.rem(d, 2)]

    def fill(o, start, arrived=None):
        @pl.loop(0, 6)
        def _(n):
            where, rows = wanted(plane[o], start + n)
            if arrived is not None:
                rows = lax.select(where == t, rows, arrived[n])
            hold[o - 1, start + n] = rows

    @step((ZF,))
    def _():
        roots.finish()
        fill(2, 0)
        fill(2, 6)
        kept["z", 0] = [
            net.start(hold.at[1, first_k], far_in.at[0], right),
            net.start(hold.at[1, last_k], far_in.at[1], left),
        ]

    @step((ZP,))
    def _():
        fill(1, 6)
        fill(3, 0)
        kept["z", 1] = [
            net.start(hold.at[0, last_k], plain_in.at[0], right),
            net.start(hold.at[2, first_k], plain_in.at[1], left),
        ]

    @step((ZM, 0))
    def _():
        kept["z", 0][0].wait_recv()
        fill(1, 0, far_in.at[0])
        kept["z", 2] = net.start(hold.at[0, first_k], merged_in.at[0], right)

    @step((ZM, 1))
    def _():
        kept["z", 0][1].wait_recv()
        fill(3, 6, far_in.at[1])
        kept["z", 3] = net.start(hold.at[2, last_k], merged_in.at[1], left)

    root_send, root_mid = v["root_send"], v["root_mid"]

    @step((ZSEL,))
    def _():
        for copy in kept["z", 1] + [kept["z", 2], kept["z", 3]]:
            copy.wait_recv()
        for side in range(2):
            for block in range(6):
                where, rows = wanted(t, side * 6 + block)
                away = wrap(where - t)
                if side == 0:
                    other_rows = lax.select(away == 1, plain_in[1, block], merged_in[0, block])
                else:
                    other_rows = lax.select(away == 3, plain_in[0, block], merged_in[1, block])
                rows = lax.select(away == 0, rows, other_rows)
                for s in range(2):
                    line, rank = spot(s, block)
                    root_send[s, line, side, rank] = rows[s]

    g_send, g_mid = v["g_send"], v["g_mid"]

    def sum_up(s):
        sums.finish(s, g)
        here, there = g.at[:, s], every[s].at[t]
        kept["g", s] = [net.start(here, there, right), net.start(here, there, left)]
        kept["g_own", s] = net.local(here, there)

    def pass_along(s, way):
        kept["g", s][way].wait_recv()
        rows = every[s].at[plane[3], lo] if way == 0 else every[s].at[plane[1], hi]
        kept["g_pass", s, way] = net.start(rows, rows, right if way == 0 else left)

    def send_g(s):
        for block in range(6):
            line, rank = spot(s, block)
            g_send[s, line, 0, rank] = g[block, s]
        kept["gl", s] = WorkerLeg(net, s, g_send.at[s], g_mid.at[s], v["g_relay"].at[s])

    def send_roots(s):
        kept["rl", s] = WorkerLeg(net, s, root_send.at[s], root_mid.at[s], v["r_relay"].at[s])

    mats = v["mats"]

    def gather(name, leg, s, mid, first, count, relay):
        def land(j, h):
            if s == 0:
                return mats.at[pl.ds(first, count), half(h), j, c, 0]
            return mats.at[pl.ds(first, count), j, half(h), c, 1]

        kept[leg, s].finish()
        kept[name, s] = Gather(workers, s, lambda rank, h: mid.at[s, :, half(h), rank], land, relay.at[s])

    shares = [net.make(mats.at[m, :, :, c], mats.at[m, :, :, c], net.pair) for m in (2, 1)]
    net.open += [(copy, workers.is_worker) for copy in shares]
    mixed, result = v["mixed"], v["result"]

    def share(name, k):
        @pl.when(workers.is_worker)
        def _():
            for s in range(2):
                kept[name, s].wait_here()
            shares[k].start()

    def column_tiles(function):
        @pl.loop(0, 4)
        def _(n):
            function(pl.ds(pl.multiple_of(n * 256, 256), 256))

    @step((MMA,))
    def _():
        @pl.when(workers.is_worker)
        def _():
            shares[0].wait_recv()

            @column_tiles
            def _(cols):
                block = mats[2, :, :, :, :, :, cols].reshape(1024, 256)
                rows = mats[0, :, :, c].reshape(512, 1024)
                mixed[:, cols] = jnp.dot(rows, block, preferred_element_type=f32).astype(bf16)

    @step((MMB,))
    def _():
        @pl.when(workers.is_worker)
        def _():
            shares[1].wait_recv()

            @column_tiles
            def _(cols):
                block = mats[1, :, :, :, :, :, cols].reshape(1024, 256)
                rows = jnp.dot(mixed[...], block, preferred_element_type=f32).astype(bf16)
                result[:, :, :, :, cols] = rows.reshape(4, 4, 2, 16, 256)

    back, home = v["back"], v["home"]

    @step((SP,))
    def _():
        for s in range(2):
            kept["sp", s] = Spread(
                workers,
                s,
                lambda j, h, s=s: result.at[half(h), j, 0] if s == 0 else result.at[j, half(h), 1],
                lambda rank, h, s=s: back.at[s, rank, half(h)],
                v["u_relay"].at[s],
            )

    def go_home(s):
        kept["sp", s].finish()
        kept["ul", s] = HomeLeg(net, s, back.at[s], home.at[s], v["u_relay2"].at[s])

    @step((ULE,))
    def _():
        for s in range(2):
            kept["ul", s].finish()
            for block in range(6):
                line, rank = spot(s, block)
                v["update"][block, s] = home[s, line, rank]

    steps[(OWE,)] = owned.finish
    steps[(SH0,)] = functools.partial(share, "gg", 0)
    steps[(SH1,)] = functools.partial(share, "rg", 1)
    for s in range(2):
        bind = functools.partial
        steps[RO1, s] = bind(roots.first, s)
        steps[RO2, s] = bind(roots.second, s)
        steps[OW1, s] = bind(pack_owned, s)
        steps[OW2, s] = bind(owned.second, s)
        steps[FAR, s] = bind(sums.far, s)
        steps[SEC, s] = bind(sums.second, s)
        steps[G, s] = bind(sum_up, s)
        steps[GL, s] = bind(send_g, s)
        steps[RL, s] = bind(send_roots, s)
        steps[GG, s] = bind(gather, "gg", "gl", s, g_mid, 2, 1, v["g_relay2"])
        steps[RG, s] = bind(gather, "rg", "rl", s, root_mid, 0, 2, v["r_relay2"])
        steps[GGF, s] = lambda s=s: kept["gg", s].forward()
        steps[RGF, s] = lambda s=s: kept["rg", s].forward()
        steps[SPF, s] = lambda s=s: kept["sp", s].forward()
        steps[UL, s] = bind(go_home, s)
        for way in range(2):
            steps[PLAIN, way, s] = bind(sums.plain, way, s)
            steps[MERGED, way, s] = bind(sums.merged, way, s)
            steps[SECP, way, s] = bind(sums.second_plain, way, s)
            steps[SECM, way, s] = bind(sums.second_merged, way, s)
            steps[ZAF, s, way] = bind(pass_along, s, way)
            for name, trip, leg in ((RO1F, roots, 0), (RO2F, roots, 1), (OW1F, owned, 0), (OW2F, owned, 1)):
                steps[name, s, way] = (
                    lambda trip=trip, leg=leg, s=s, way=way: trip.legs[leg, s].forward(way)
                )
            for name, leg in ((GLF, "gl"), (RLF, "rl"), (ULF, "ul")):
                steps[name, s, way] = lambda leg=leg, s=s, way=way: kept[leg, s].forward(way)
    assert sorted(steps) == sorted(ORDER)
    for name in ORDER:
        steps[name]()
    net.close()


def step(grads, owner_slots, root):
    tile = (16, root.shape[1])
    vmem = {
        "own": (2, 4, 6, 4),
        "cin": (2, 4, 6, 4),
        "first_in": (3, 2, 2, 3, 4),
        "f": (2, 4, 6),
        "second_in": (3, 2, 2, 3),
        "g": (6, 2),
        "every_0": (4, 6),
        "every_1": (4, 6),
        "root_middle": (2, 4, 4, 2),
        "root_relay": (2, 2, 2, 2, 2),
        "roots": (4, 4, 2, 2),
        "g_send": (2, 4, 1, 2),
        "g_mid": (2, 1, 4, 2),
        "g_relay2": (2, 2, 1, 2),
        "mats": (3, 4, 4, 2, 2),
        "owned_parcels": (2, 4, 4, 2),
        "owned_middle": (2, 4, 4, 2),
        "owned_relay": (2, 2, 2, 2, 2),
        "hold": (3, 12, 2),
        "z_far": (2, 6, 2),
        "z_plain": (2, 6, 2),
        "z_merged": (2, 6, 2),
        "root_send": (2, 4, 2, 2),
        "root_mid": (2, 2, 4, 2),
        "r_relay2": (2, 2, 2, 2),
        "result": (4, 4, 2),
        "back": (2, 2, 4),
        "home": (2, 4, 2),
        "u_relay": (2, 2, 2),
    }
    scratch = {name: pltpu.VMEM(shape + tile, bf16) for name, shape in vmem.items()}
    scratch["g_relay"] = pltpu.VMEM((2, 2, 1, 2, 16, tile[1] // 2), bf16)
    scratch["r_relay"] = pltpu.VMEM((2, 2, 2, 2, 16, tile[1] // 2), bf16)
    scratch["u_relay2"] = pltpu.VMEM((2, 2, 2, 16, tile[1] // 2), bf16)
    scratch["mixed"] = pltpu.VMEM((512, tile[1]), bf16)
    scratch["blocks"] = pltpu.SMEM((32,), jnp.int32)
    scratch["send"] = pltpu.SemaphoreType.DMA((288,))
    scratch["recv"] = pltpu.SemaphoreType.DMA((288,))
    names = ["parts", "owners", "root", "owned", "update"] + list(scratch)
    in_vmem = pl.BlockSpec(memory_space=pltpu.VMEM)
    anywhere = pl.BlockSpec(memory_space=pl.ANY)
    owned, update = pl.pallas_call(
        functools.partial(step_kernel, names),
        out_shape=(
            jax.ShapeDtypeStruct((4, 4, 2, 2) + tile, bf16),
            jax.ShapeDtypeStruct((6, 2) + tile, bf16),
        ),
        in_specs=[anywhere, pl.BlockSpec(memory_space=pltpu.SMEM), anywhere],
        out_specs=(anywhere, in_vmem),
        scratch_shapes=list(scratch.values()),
        compiler_params=pltpu.CompilerParams(
            collective_id=0, has_side_effects=True, vmem_limit_bytes=62 * 2**20
        ),
    )(grads.reshape((6, 4, 4, 2, 2) + tile), owner_slots, root.reshape((4, 4, 2, 2) + tile))
    return owned.reshape(1024, tile[1]), update.reshape(6, 32, tile[1])


def stats_kernel(owners, block_ref, old_ref, update, new_ref, update_out, block, turned, stats, held, sem):
    me = lax.axis_index("dp") * 4 + lax.axis_index("tensor")
    parts = [pl.ds(256 * i, 256) for i in range(4)]
    copy = pltpu.make_async_copy
    fetches = [copy(block_ref.at[parts[i]], block.at[parts[i]], sem.at[i]) for i in range(4)]
    loads = [copy(old_ref.at[parts[i]], stats.at[parts[i]], sem.at[4 + i]) for i in range(4)]
    stores = [copy(stats.at[parts[i]], new_ref.at[parts[i]], sem.at[8 + i]) for i in range(4)]
    take, give = copy(update, held, sem.at[12]), copy(held, update_out, sem.at[13])
    for each in fetches + [take] + loads:
        each.start()
    is_left, is_right = owners[0, 0] == me, owners[1, 0] == me
    for b in range(1, 24):
        is_left = jnp.logical_or(is_left, owners[0, b] == me)
        is_right = jnp.logical_or(is_right, owners[1, b] == me)
    named = jnp.logical_or(is_left, is_right)

    def turn(part):
        turned[:, part] = block[part, :].T

    for i in range(4):
        fetches[i].wait()
        pl.when(named)(functools.partial(turn, parts[i]))
    take.wait()
    give.start()

    def blend(part, rows, other):
        gram = jnp.dot(rows[part, :], other[...], preferred_element_type=f32)
        stats[part, :] = decay_rate * stats[part, :] + (1 - decay_rate) * (gram * block.shape[1] ** (-0.5))

    for i in range(4):
        loads[i].wait()
        pl.when(is_left)(functools.partial(blend, parts[i], block, turned))
        pl.when(is_right)(functools.partial(blend, parts[i], turned, block))
        stores[i].start()
    for each in stores + [give]:
        each.wait()


def finish_stats(owner_slots, block, old, update):
    anywhere = pl.BlockSpec(memory_space=pl.ANY)
    return pl.pallas_call(
        stats_kernel,
        out_shape=(
            jax.ShapeDtypeStruct(old.shape, f32),
            jax.ShapeDtypeStruct(update.shape, bf16),
        ),
        in_specs=[pl.BlockSpec(memory_space=pltpu.SMEM), anywhere, anywhere, anywhere],
        out_specs=(anywhere, anywhere),
        scratch_shapes=[
            pltpu.VMEM(block.shape, bf16),
            pltpu.VMEM(block.shape, bf16),
            pltpu.VMEM(old.shape, f32),
            pltpu.VMEM(update.shape, bf16),
            pltpu.SemaphoreType.DMA((14,)),
        ],
        compiler_params=pltpu.CompilerParams(vmem_limit_bytes=60 * 2**20),
    )(owner_slots, block, old, update)


def body(partial_grads, owner_slots, statistics, inv_roots):
    owners = owner_slots.T
    owned, update = step(partial_grads[0], owners, inv_roots[0, 0, 0])
    new_stats, update = finish_stats(owners, owned, statistics[0, 0, 0], update)
    return (new_stats[None, None, None], update)


def solution(mesh):
    return jax.shard_map(
        body,
        mesh=mesh,
        in_specs=(
            P("dp", "tensor", None, None),
            P(),
            P("dp", "tensor", None, None, None),
            P("dp", "tensor", None, None, None),
        ),
        out_specs=(P("dp", "tensor", None, None, None), P("tensor", "dp", None)),
        check_vma=False,
    )
```

```python
import functools

import jax
import jax.numpy as jnp
from jax import lax
from jax.experimental import pallas as pl
from jax.experimental.pallas import tpu as pltpu
from jax.sharding import PartitionSpec as P

decay_rate = 0.9
MESH = pl.DeviceIdType.MESH
f32 = jnp.float32
bf16 = jnp.bfloat16
lo, hi = pl.ds(0, 3), pl.ds(3, 3)


def place():
    d = lax.axis_index("dp")
    return lax.div(d, 8), lax.rem(lax.div(d, 2), 4), lax.rem(d, 2), lax.axis_index("tensor")


def wrap(v):
    return lax.rem(v + 8, 4)


def remote(src, dst, send, recv, device):
    return pltpu.make_async_remote_copy(
        src_ref=src, dst_ref=dst, send_sem=send, recv_sem=recv, device_id=device, device_id_type=MESH
    )


class Net:
    def __init__(self, send, recv):
        self.x, self.y, self.c, self.t = place()
        self.send, self.recv, self.count, self.open = send, recv, 0, []
        self.at = {"x": self.x, "y": self.y, "z": self.t}
        self.pair = ((self.x * 4 + self.y) * 2 + 1 - self.c, self.t)

    def near(self, axis, step, swap=0):
        x, y, t = [wrap(self.at[a] + step) if a == axis else self.at[a] for a in "xyz"]
        return ((x * 4 + y) * 2 + (1 - self.c if swap else self.c), t)

    def greet(self):
        barrier = pltpu.get_barrier_semaphore()
        peers = [self.pair] + [self.near(axis, step) for axis in "xyz" for step in (1, -1)]
        peers += [self.near(axis, step, 1) for axis in "xy" for step in (1, -1)]
        for peer in peers:
            pl.semaphore_signal(barrier, inc=1, device_id=peer, device_id_type=MESH)
        pl.semaphore_wait(barrier, len(peers))

    def make(self, src, dst, device):
        copy = remote(src, dst, self.send.at[self.count], self.recv.at[self.count], device)
        self.count += 1
        return copy

    def start(self, src, dst, device, when=None):
        copy = self.make(src, dst, device)
        if when is None:
            copy.start()
        else:
            pl.when(when)(copy.start)
        self.open.append((copy, when))
        return copy

    def local(self, src, dst):
        copy = pltpu.make_async_copy(src, dst, self.send.at[self.count])
        self.count += 1
        copy.start()
        return copy

    def close(self, count):
        for copy, when in self.open[:count]:
            if when is None:
                copy.wait_send()
            else:
                pl.when(when)(copy.wait_send)
        self.open = self.open[count:]


class Exchange:
    def __init__(self, net, axis, src, dst, relay):
        self.net, self.axis, self.dst, self.relay = net, axis, dst, relay
        here = net.at[axis]
        self.i = [wrap(here + o) for o in range(4)]
        right, left = net.near(axis, 1), net.near(axis, -1)
        self.far = [
            net.start(src(self.i[2], 0), relay.at[0], right),
            net.start(src(self.i[2], 1), relay.at[1], left),
        ]
        self.own = net.local(src(self.i[0], None), dst(self.i[0], None))
        self.direct = [
            net.start(src(self.i[1], None), dst(self.i[0], None), right),
            net.start(src(self.i[3], None), dst(self.i[0], None), left),
        ]

        self.passed = []

    def forward(self, way):
        self.far[way].wait_recv()
        source = self.i[3 if way == 0 else 1]
        self.passed.append(
            self.net.start(self.relay.at[way], self.dst(source, way), self.net.near(self.axis, 1 - 2 * way))
        )

    def finish(self):
        self.own.wait()
        for copy in self.direct + self.passed:
            copy.wait_recv()


def half(h):
    return slice(None) if h is None else pl.ds(2 * h, 2)


class LastLeg:
    def __init__(self, net, axis, src, dst, relay):
        self.net, self.axis, self.dst, self.relay = net, axis, dst, relay
        here = net.at[axis]
        self.i = [wrap(here + o) for o in range(4)]
        self.cores = [net.c, 1 - net.c]
        every = slice(None)
        self.far = [
            net.start(src(self.i[2], way, every), relay.at[way], net.near(axis, 1 - 2 * way)) for way in range(2)
        ]
        self.arrive = [
            net.start(src(self.i[o], None, self.cores[k]), dst(self.i[0], None), net.near(axis, step, k))
            for o, step in ((1, 1), (3, -1))
            for k in range(2)
        ]
        self.own = net.local(src(self.i[0], None, self.cores[0]), dst(self.i[0], None))
        self.arrive.append(net.start(src(self.i[0], None, self.cores[1]), dst(self.i[0], None), net.pair))

    def forward(self, way):
        net = self.net
        source = self.i[3 if way == 0 else 1]
        self.far[way].wait_recv()
        self.arrive += [
            net.start(
                self.relay.at[way, :, self.cores[k]], self.dst(source, way), net.near(self.axis, 1 - 2 * way, k)
            )
            for k in range(2)
        ]

    def finish(self):
        self.own.wait()
        for copy in self.arrive:
            copy.wait_recv()


class PlaneExchange:
    def __init__(self, net, parcels, middle, landing, relay):
        self.net, self.parcels, self.middle, self.landing, self.relay = net, parcels, middle, landing, relay
        self.legs = {}

    def first(self, s):
        a, d = self.parcels, self.middle

        def parcels(i, h):
            return a(0, i, half(h)) if s == 0 else a(1, half(h), i)

        self.legs[0, s] = Exchange(
            self.net, "xy"[s], parcels, lambda i, h: d.at[s, i, half(h)], self.relay.at[0, s]
        )

    def second(self, s):
        d, z, c = self.middle, self.landing, self.net.c
        self.legs[0, s].finish()

        def land(j, h):
            return z.at[half(h), j, c, 0] if s == 0 else z.at[j, half(h), c, 1]

        self.legs[1, s] = LastLeg(
            self.net, "yx"[s], lambda j, h, k: d.at[s, half(h), j, k], land, self.relay.at[1, s]
        )

    def finish(self):
        for s in range(2):
            self.legs[1, s].finish()


class WorkerLeg:
    def __init__(self, net, s, source, target, relay):
        self.net, self.s, self.axis = net, s, "xy"[s]
        here = net.at[self.axis]
        self.target, self.relay = target, relay
        self.i = i = [wrap(here + o) for o in range(4)]
        self.two = [v < 2 if s == 0 else v >= 2 for v in i]
        wide = relay.shape[-1]
        self.cols = [pl.ds(0, wide), pl.ds(wide, wide)]

        def when(o, rank):
            return self.two[o] if rank else None

        self.when = when
        self.far = [
            [
                net.start(
                    source.at[i[2], :, rank, :, self.cols[way]],
                    relay.at[way, :, rank],
                    net.near(self.axis, 1 - 2 * way),
                    when(2, rank),
                )
                for way in range(2)
            ]
            for rank in range(2)
        ]
        self.direct = [
            [
                net.start(
                    source.at[i[o], :, rank], target.at[:, i[0], rank], net.near(self.axis, step), when(o, rank)
                )
                for o, step in ((1, 1), (3, -1))
            ]
            for rank in range(2)
        ]
        self.own = net.local(source.at[i[0]], target.at[:, i[0]])
        self.passed = [[], []]

    def forward(self, way):
        o, goal = ((3, 1), (1, 3))[way]
        for rank in range(2):
            arrived = self.far[rank][way]
            when = self.when(goal, rank)
            if when is None:
                arrived.wait_recv()
            else:
                pl.when(when)(arrived.wait_recv)
            self.passed[rank].append(
                self.net.start(
                    self.relay.at[way, :, rank],
                    self.target.at[:, self.i[o], rank, :, self.cols[way]],
                    self.net.near(self.axis, 1 - 2 * way),
                    when,
                )
            )

    def finish(self):
        self.own.wait()
        for copy in self.direct[0] + self.passed[0]:
            copy.wait_recv()

        @pl.when(self.two[0])
        def _():
            for copy in self.direct[1] + self.passed[1]:
                copy.wait_recv()


class HomeLeg:
    def __init__(self, net, s, back, home, relay):
        self.net, self.axis, self.home, self.relay = net, "xy"[s], home, relay
        here = net.at[self.axis]
        self.i = i = [wrap(here + o) for o in range(4)]
        self.two = [v < 2 if s == 0 else v >= 2 for v in i]
        wide = relay.shape[-1]
        self.cols = [pl.ds(0, wide), pl.ds(wide, wide)]
        self.far = [
            [
                net.start(
                    back.at[rank, i[2], :, self.cols[way]],
                    relay.at[way, rank],
                    net.near(self.axis, 1 - 2 * way),
                    self.when(0, rank),
                )
                for way in range(2)
            ]
            for rank in range(2)
        ]
        self.direct = [
            [
                net.start(back.at[rank, i[o]], home.at[i[0], rank], net.near(self.axis, step), self.when(0, rank))
                for o, step in ((1, 1), (3, -1))
            ]
            for rank in range(2)
        ]
        self.own = net.local(back.at[:, i[0]], home.at[i[0]])
        self.passed = [[], []]

    def when(self, o, rank):
        return self.two[o] if rank else None

    def arrived(self, copy, o, rank):
        if rank:
            pl.when(self.two[o])(copy.wait_recv)
        else:
            copy.wait_recv()

    def forward(self, way):
        o = (3, 1)[way]
        for rank in range(2):
            self.arrived(self.far[rank][way], o, rank)
            self.passed[rank].append(
                self.net.start(
                    self.relay.at[way, rank],
                    self.home.at[self.i[o], rank, :, self.cols[way]],
                    self.net.near(self.axis, 1 - 2 * way),
                    self.when(o, rank),
                )
            )

    def finish(self):
        self.own.wait()
        for rank in range(2):
            for copy, o in zip(self.direct[rank] + self.passed[rank], (3, 1, 2, 2)):
                self.arrived(copy, o, rank)


def spot(s, block):
    if block < 4:
        return block, 0
    return (block - 4, 1) if s == 0 else (block - 2, 1)


class Workers:
    def __init__(self, net):
        self.net = net
        self.is_worker = lax.rem(net.x - net.y + 4, 2) == 0
        self.is_other = lax.rem(net.x - net.y + 4, 2) == 1
        self.ij = [(net.x, net.y), (net.y, net.x)]
        self.axes = ["y", "x"]

    def rank(self, s, step):
        i, j = self.ij[s]
        return lax.div(wrap(j + step - i), 2)

    def beside(self, s):
        return self.net.near(self.axes[s], 1), self.net.near(self.axes[s], -1)


class Gather:
    def __init__(self, w, s, unit, land, relay):
        self.w, net = w, w.net
        right, left = w.beside(s)
        j = [wrap(w.ij[s][1] + o) for o in range(4)]
        self.far = [
            net.make(unit(w.rank(s, 2), 0), relay.at[0], right),
            net.make(unit(w.rank(s, 2), 1), relay.at[1], left),
        ]
        self.direct = [
            net.make(unit(w.rank(s, 1), None), land(j[0], None), right),
            net.make(unit(w.rank(s, 3), None), land(j[0], None), left),
        ]
        self.passed = [
            net.make(relay.at[0], land(j[3], 0), right),
            net.make(relay.at[1], land(j[1], 1), left),
        ]
        self.own = pltpu.make_async_copy(unit(w.rank(s, 0), None), land(j[0], None), net.send.at[net.count])
        net.count += 1

        @pl.when(w.is_worker)
        def _():
            for copy in self.far + [self.own]:
                copy.start()

        @pl.when(w.is_other)
        def _():
            for copy in self.direct:
                copy.start()

        net.open += [(copy, w.is_worker) for copy in self.far]
        net.open += [(copy, w.is_other) for copy in self.direct + self.passed]

    def forward(self):
        @pl.when(self.w.is_other)
        def _():
            for arrived, onward in zip(self.far, self.passed):
                arrived.wait_recv()
                onward.start()

    def wait_here(self):
        self.own.wait()
        for copy in self.direct + self.passed:
            copy.wait_recv()


class Spread:
    def __init__(self, w, s, unit, land, relay):
        self.w, net = w, w.net
        right, left = w.beside(s)
        j = [wrap(w.ij[s][1] + o) for o in range(4)]
        mine = w.rank(s, 0)
        self.far = [net.make(unit(j[2], 0), relay.at[0], right), net.make(unit(j[2], 1), relay.at[1], left)]
        self.direct = [
            net.make(unit(j[1], None), land(mine, None), right),
            net.make(unit(j[3], None), land(mine, None), left),
        ]
        self.passed = [
            net.make(relay.at[0], land(w.rank(s, 3), 0), right),
            net.make(relay.at[1], land(w.rank(s, 1), 1), left),
        ]
        self.own = pltpu.make_async_copy(unit(j[0], None), land(mine, None), net.send.at[net.count])
        net.count += 1

        @pl.when(w.is_worker)
        def _():
            for copy in self.far + self.direct + [self.own]:
                copy.start()

        net.open += [(copy, w.is_worker) for copy in self.far + self.direct]
        net.open += [(copy, w.is_other) for copy in self.passed]

    def forward(self):
        @pl.when(self.w.is_other)
        def _():
            for arrived, onward in zip(self.far, self.passed):
                arrived.wait_recv()
                onward.start()

    def finish(self):
        @pl.when(self.w.is_other)
        def _():
            for copy in self.direct:
                copy.wait_recv()

        @pl.when(self.w.is_worker)
        def _():
            self.own.wait()
            for copy in self.passed:
                copy.wait_recv()


class ReduceScatter:
    def __init__(self, net, parts, v):
        self.net, self.parts, self.v = net, parts, v
        at = [(net.x, net.y), (net.y, net.x)]
        self.i = [[wrap(at[s][0] + o) for o in range(4)] for s in range(2)]
        self.j = [[wrap(at[s][1] + o) for o in range(4)] for s in range(2)]
        self.loads, self.swaps, self.copies = {}, {}, {}

    def fetch(self, order):
        net, own, cin = self.net, self.v["own"], self.v["cin"]

        def view(s, i, core):
            return self.parts.at[:, i, :, core, 0] if s == 0 else self.parts.at[:, :, i, core, 1]

        for o in order:
            for s in range(2):
                i = self.i[s][o]
                self.swaps[s, o] = net.start(view(s, i, 1 - net.c), cin.at[s, i], net.pair)
                self.loads[s, o] = net.local(view(s, i, net.c), own.at[s, i])

    def ship(self, stage, s, way, src, dst):
        axis = "xy"[s] if stage < 3 else "yx"[s]
        self.copies[stage, s, way] = self.net.start(src, dst, self.net.near(axis, 1 - 2 * way))

    def ready(self, s, o):
        self.loads[s, o].wait()
        self.swaps[s, o].wait_recv()

    def add(self, out, terms, blocks):
        @pl.loop(0, blocks)
        def _(b):
            for j in range(4):
                total = terms[0][b, j].astype(f32)
                for term in terms[1:]:
                    total = total + term[b, j].astype(f32)
                out[b, j] = total.astype(bf16)

    def far(self, s):
        own, cin, first_in = self.v["own"], self.v["cin"], self.v["first_in"]
        i = self.i[s][2]
        self.ready(s, 2)
        self.add(own.at[s, i], [own.at[s, i], cin.at[s, i]], 6)
        self.ship(0, s, 0, own.at[s, i, lo], first_in.at[0, s, 0])
        self.ship(0, s, 1, own.at[s, i, hi], first_in.at[0, s, 1])

    def plain(self, way, s):
        own, cin, first_in = self.v["own"], self.v["cin"], self.v["first_in"]
        o, part = ((1, hi), (3, lo))[way]
        i = self.i[s][o]
        self.ready(s, o)
        self.add(own.at[s, i, part], [own.at[s, i, part], cin.at[s, i, part]], 3)
        self.ship(1, s, way, own.at[s, i, part], first_in.at[1, s, way])

    def merged(self, way, s):
        own, cin, first_in = self.v["own"], self.v["cin"], self.v["first_in"]
        o, part = ((1, lo), (3, hi))[way]
        i = self.i[s][o]
        self.copies[0, s, way].wait_recv()
        terms = [own.at[s, i, part], cin.at[s, i, part], first_in.at[0, s, way]]
        self.add(own.at[s, i, part], terms, 3)
        self.ship(2, s, way, own.at[s, i, part], first_in.at[2, s, way])

    def first_sum(self, s, j, b):
        own, cin, first_in = self.v["own"], self.v["cin"], self.v["first_in"]
        i = self.i[s][0]
        total = own[s, i, b, j].astype(f32) + cin[s, i, b, j].astype(f32)
        k, low = (b, 0) if b < 3 else (b - 3, 1)
        for stage, way in ((2, low), (1, 1 - low)):
            total = total + first_in[stage, s, way, k, j].astype(f32)
        return total

    def second(self, s):
        f, second_in = self.v["f"], self.v["second_in"]
        self.ready(s, 0)
        for stage in (1, 2):
            for way in range(2):
                self.copies[stage, s, way].wait_recv()
        j = self.j[s][2]
        for b in range(6):
            f[s, j, b] = self.first_sum(s, j, b).astype(bf16)
        self.ship(3, s, 0, f.at[s, j, lo], second_in.at[0, s, 0])
        self.ship(3, s, 1, f.at[s, j, hi], second_in.at[0, s, 1])

    def second_plain(self, way, s):
        f, second_in = self.v["f"], self.v["second_in"]
        o, part = ((1, hi), (3, lo))[way]
        j = self.j[s][o]
        for b in range(6):
            f[s, j, b] = self.first_sum(s, j, b).astype(bf16)
        self.ship(4, s, way, f.at[s, j, part], second_in.at[1, s, way])

    def second_merged(self, way, s):
        f, second_in = self.v["f"], self.v["second_in"]
        o, part, start = ((1, lo, 0), (3, hi, 3))[way]
        j = self.j[s][o]
        self.copies[3, s, way].wait_recv()
        for k in range(3):
            total = f[s, j, start + k].astype(f32) + second_in[0, s, way, k].astype(f32)
            f[s, j, start + k] = total.astype(bf16)
        self.ship(5, s, way, f.at[s, j, part], second_in.at[2, s, way])

    def finish(self, s, out):
        second_in = self.v["second_in"]
        for stage in (4, 5):
            for way in range(2):
                self.copies[stage, s, way].wait_recv()
        j = self.j[s][0]
        for b in range(6):
            total = self.first_sum(s, j, b)
            k, low = (b, 0) if b < 3 else (b - 3, 1)
            total = total + second_in[2, s, low, k].astype(f32)
            total = total + second_in[1, s, 1 - low, k].astype(f32)
            out[b, s] = total.astype(bf16)


(
    BLK, FAR, FETCH, G, GG, GGF, GL, GLF, MERGED, MMA, MMB, OW1, OW1F, OW2, OW2F, OWE, PLAIN, RG, RGF, RL, RLF,
    RO1, RO1F, RO2, RO2F, SEC, SECM, SECP, SH0, SH1, SP, SPF, UL, ULE, ULF, ZAF, ZF, ZM, ZP, ZSEL,
) = range(40)
CLOSING = (ULF, 0, 1)
RESULTS = 40
ORDER = (
    (RO1, 1), (RO1, 0), (BLK,), (RO1F, 1, 1), (RO1F, 0, 1), (RO1F, 1, 0), (RO1F, 0, 0), (FETCH,), (RO2, 1),
    (RO2, 0), (RO2F, 0, 0), (RO2F, 1, 1), (RO2F, 1, 0), (FAR, 0), (PLAIN, 0, 0), (RO2F, 0, 1), (FAR, 1), (ZF,),
    (PLAIN, 1, 0), (PLAIN, 0, 1), (PLAIN, 1, 1), (ZP,), (ZM, 1), (MERGED, 0, 1), (MERGED, 1, 0),
    (MERGED, 0, 0), (MERGED, 1, 1), (ZM, 0), (SEC, 0), (SEC, 1), (SECP, 1, 1), (SECP, 0, 0), (SECP, 1, 0),
    (SECP, 0, 1), (ZSEL,), (SECM, 0, 0), (SECM, 1, 0), (SECM, 1, 1), (SECM, 0, 1), (RL, 1), (RL, 0), (G, 0),
    (G, 1), (GL, 0), (RLF, 1, 1), (GL, 1), (RLF, 1, 0), (GLF, 1, 0), (GLF, 0, 0), (RLF, 0, 0), (GLF, 0, 1),
    (GLF, 1, 1), (RLF, 0, 1), (RG, 1), (GG, 0), (GGF, 0), (ZAF, 0, 0), (ZAF, 0, 1), (ZAF, 1, 1), (RG, 0),
    (GG, 1), (GGF, 1), (ZAF, 1, 0), (RGF, 1), (OW1, 0), (RGF, 0), (OW1, 1), (SH0,), (SH1,), (MMA,),
    (OW1F, 0, 0), (OW1F, 0, 1), (OW1F, 1, 0), (OW1F, 1, 1), (MMB,), (SP,), (SPF, 0), (SPF, 1), (OW2, 1),
    (OW2, 0), (UL, 0), (OW2F, 1, 0), (UL, 1), (ULF, 0, 1), (ULF, 1, 0), (ULF, 0, 0), (OW2F, 0, 0), (ULF, 1, 1),
    (OW2F, 1, 1), (OW2F, 0, 1), (ULE,), (OWE,),
)


def step_kernel(names, *refs):
    v = dict(zip(names, refs))
    net = Net(v["send"], v["recv"])
    t, c = net.t, net.c
    owners, g, root, blocks = v["owners"], v["g"], v["root"], v["blocks"]
    every = [v["every_0"], v["every_1"]]
    net.greet()
    right, left = net.near("z", 1), net.near("z", -1)
    plane = [wrap(t + o) for o in range(4)]
    sums = ReduceScatter(net, v["parts"], v)
    workers = Workers(net)
    steps, kept = {}, {}

    def step(name):
        def keep(function):
            steps[name] = function

        return keep

    @step((FETCH,))
    def _():
        sums.fetch((2, 1, 3, 0))

    @step((BLK,))
    def _():
        @pl.loop(0, 32)
        def _(d):
            slot, block = d * 4 + t, jnp.int32(0)
            for b in range(24):
                hit = jnp.logical_or(owners[0, b] == slot, owners[1, b] == slot)
                block = jnp.where(hit, b, block)
            blocks[d] = block

    roots = PlaneExchange(
        net, lambda s, x, y: root.at[x, y, :, s], v["root_middle"], v["roots"], v["root_relay"]
    )
    parcels = v["owned_parcels"]
    owned = PlaneExchange(
        net, lambda s, x, y: parcels.at[s, x, y], v["owned_middle"], v["results"].at[pl.ds(0, 4)], v["owned_relay"]
    )

    def pack_owned(s):
        kept["g_own", s].wait()
        for way in range(2):
            kept["g_pass", s, way].wait_recv()

        @pl.loop(0, 16)
        def _(chip):
            x, y = lax.div(chip, 4), lax.rem(chip, 4)
            for core in range(2):
                block = blocks[2 * chip + core]
                parcels[s, x, y, core] = every[s][lax.div(block, 6), lax.rem(block, 6)]

        owned.first(s)

    pieces, hold = v["roots"], v["hold"]
    far_in, plain_in, merged_in = v["z_far"], v["z_plain"], v["z_merged"]
    first_k, last_k = pl.ds(0, 6), pl.ds(6, 6)

    def wanted(target, k):
        slot = owners[lax.div(k, 6), target * 6 + lax.rem(k, 6)]
        d = lax.div(slot, 4)
        return lax.rem(slot, 4), pieces[lax.div(d, 8), lax.rem(lax.div(d, 2), 4), lax.rem(d, 2)]

    def fill(o, start, arrived=None):
        @pl.loop(0, 6)
        def _(n):
            where, rows = wanted(plane[o], start + n)
            if arrived is not None:
                rows = lax.select(where == t, rows, arrived[n])
            hold[o - 1, start + n] = rows

    @step((ZF,))
    def _():
        roots.finish()
        fill(2, 0)
        fill(2, 6)
        kept["z", 0] = [
            net.start(hold.at[1, first_k], far_in.at[0], right),
            net.start(hold.at[1, last_k], far_in.at[1], left),
        ]

    @step((ZP,))
    def _():
        fill(1, 6)
        fill(3, 0)
        kept["z", 1] = [
            net.start(hold.at[0, last_k], plain_in.at[0], right),
            net.start(hold.at[2, first_k], plain_in.at[1], left),
        ]

    @step((ZM, 0))
    def _():
        kept["z", 0][0].wait_recv()
        fill(1, 0, far_in.at[0])
        kept["z", 2] = net.start(hold.at[0, first_k], merged_in.at[0], right)

    @step((ZM, 1))
    def _():
        kept["z", 0][1].wait_recv()
        fill(3, 6, far_in.at[1])
        kept["z", 3] = net.start(hold.at[2, last_k], merged_in.at[1], left)

    root_send, root_mid = v["root_send"], v["root_mid"]

    @step((ZSEL,))
    def _():
        for copy in kept["z", 1] + [kept["z", 2], kept["z", 3]]:
            copy.wait_recv()
        for side in range(2):
            for block in range(6):
                where, rows = wanted(t, side * 6 + block)
                away = wrap(where - t)
                if side == 0:
                    other_rows = lax.select(away == 1, plain_in[1, block], merged_in[0, block])
                else:
                    other_rows = lax.select(away == 3, plain_in[0, block], merged_in[1, block])
                rows = lax.select(away == 0, rows, other_rows)
                for s in range(2):
                    line, rank = spot(s, block)
                    root_send[s, line, side, rank] = rows[s]

    g_send, g_mid = v["g_send"], v["g_mid"]

    def sum_up(s):
        sums.finish(s, g)
        here, there = g.at[:, s], every[s].at[t]
        kept["g", s] = [net.start(here, there, right), net.start(here, there, left)]
        kept["g_own", s] = net.local(here, there)

    def pass_along(s, way):
        kept["g", s][way].wait_recv()
        rows = every[s].at[plane[3], lo] if way == 0 else every[s].at[plane[1], hi]
        kept["g_pass", s, way] = net.start(rows, rows, right if way == 0 else left)

    def send_g(s):
        for block in range(6):
            line, rank = spot(s, block)
            g_send[s, line, 0, rank] = g[block, s]
        kept["gl", s] = WorkerLeg(net, s, g_send.at[s], g_mid.at[s], v["g_relay"].at[s])

    def send_roots(s):
        kept["rl", s] = WorkerLeg(net, s, root_send.at[s], root_mid.at[s], v["r_relay"].at[s])

    mats = v["mats"]

    def gather(name, leg, s, mid, first, count, relay):
        def land(j, h):
            if s == 0:
                return mats.at[pl.ds(first, count), half(h), j, c, 0]
            return mats.at[pl.ds(first, count), j, half(h), c, 1]

        kept[leg, s].finish()
        kept[name, s] = Gather(workers, s, lambda rank, h: mid.at[s, :, half(h), rank], land, relay.at[s])

    shares = [net.make(mats.at[m, :, :, c], mats.at[m, :, :, c], net.pair) for m in (2, 1)]
    net.open += [(copy, workers.is_worker) for copy in shares]
    mixed, result = v["mixed"], v["result"]

    def share(name, k):
        @pl.when(workers.is_worker)
        def _():
            for s in range(2):
                kept[name, s].wait_here()
            shares[k].start()

    def column_tiles(function):
        @pl.loop(0, 4)
        def _(n):
            function(pl.ds(pl.multiple_of(n * 256, 256), 256))

    @step((MMA,))
    def _():
        @pl.when(workers.is_worker)
        def _():
            shares[0].wait_recv()

            @column_tiles
            def _(cols):
                block = mats[2, :, :, :, :, :, cols].reshape(1024, 256)
                rows = mats[0, :, :, c].reshape(512, 1024)
                mixed[:, cols] = jnp.dot(rows, block, preferred_element_type=f32).astype(bf16)

    @step((MMB,))
    def _():
        @pl.when(workers.is_worker)
        def _():
            shares[1].wait_recv()

            @column_tiles
            def _(cols):
                block = mats[1, :, :, :, :, :, cols].reshape(1024, 256)
                rows = jnp.dot(mixed[...], block, preferred_element_type=f32).astype(bf16)
                result[:, :, :, :, cols] = rows.reshape(4, 4, 2, 16, 256)

    back, home = v["back"], v["home"]

    @step((SP,))
    def _():
        for s in range(2):
            kept["sp", s] = Spread(
                workers,
                s,
                lambda j, h, s=s: result.at[half(h), j, 0] if s == 0 else result.at[j, half(h), 1],
                lambda rank, h, s=s: back.at[s, rank, half(h)],
                v["u_relay"].at[s],
            )

    def go_home(s):
        kept["sp", s].finish()
        kept["ul", s] = HomeLeg(net, s, back.at[s], home.at[s], v["u_relay2"].at[s])

    @step((ULE,))
    def _():
        for s in range(2):
            kept["ul", s].finish()
            for block in range(6):
                line, rank = spot(s, block)
                v["update"][block // 2, block % 2, s] = home[s, line, rank]
        kept["update"] = net.local(v["update"], v["results"].at[4, pl.ds(0, 3)])

    steps[(OWE,)] = owned.finish
    steps[(SH0,)] = functools.partial(share, "gg", 0)
    steps[(SH1,)] = functools.partial(share, "rg", 1)
    for s in range(2):
        bind = functools.partial
        steps[RO1, s] = bind(roots.first, s)
        steps[RO2, s] = bind(roots.second, s)
        steps[OW1, s] = bind(pack_owned, s)
        steps[OW2, s] = bind(owned.second, s)
        steps[FAR, s] = bind(sums.far, s)
        steps[SEC, s] = bind(sums.second, s)
        steps[G, s] = bind(sum_up, s)
        steps[GL, s] = bind(send_g, s)
        steps[RL, s] = bind(send_roots, s)
        steps[GG, s] = bind(gather, "gg", "gl", s, g_mid, 2, 1, v["g_relay2"])
        steps[RG, s] = bind(gather, "rg", "rl", s, root_mid, 0, 2, v["r_relay2"])
        steps[GGF, s] = lambda s=s: kept["gg", s].forward()
        steps[RGF, s] = lambda s=s: kept["rg", s].forward()
        steps[SPF, s] = lambda s=s: kept["sp", s].forward()
        steps[UL, s] = bind(go_home, s)
        for way in range(2):
            steps[PLAIN, way, s] = bind(sums.plain, way, s)
            steps[MERGED, way, s] = bind(sums.merged, way, s)
            steps[SECP, way, s] = bind(sums.second_plain, way, s)
            steps[SECM, way, s] = bind(sums.second_merged, way, s)
            steps[ZAF, s, way] = bind(pass_along, s, way)
            for name, trip, leg in ((RO1F, roots, 0), (RO2F, roots, 1), (OW1F, owned, 0), (OW2F, owned, 1)):
                steps[name, s, way] = (
                    lambda trip=trip, leg=leg, s=s, way=way: trip.legs[leg, s].forward(way)
                )
            for name, leg in ((GLF, "gl"), (RLF, "rl"), (ULF, "ul")):
                steps[name, s, way] = lambda leg=leg, s=s, way=way: kept[leg, s].forward(way)
    assert sorted(steps) == sorted(ORDER)
    for name in ORDER:
        if name == (MMA,):
            early = len(net.open)
        if name == CLOSING:
            net.close(early)
        steps[name]()
    kept["update"].wait()
    net.close(len(net.open))


def step(grads, owner_slots, root):
    tile = (16, root.shape[1])
    vmem = {
        "own": (2, 4, 6, 4),
        "cin": (2, 4, 6, 4),
        "first_in": (3, 2, 2, 3, 4),
        "f": (2, 4, 6),
        "second_in": (3, 2, 2, 3),
        "g": (6, 2),
        "every_0": (4, 6),
        "every_1": (4, 6),
        "root_middle": (2, 4, 4, 2),
        "root_relay": (2, 2, 2, 2, 2),
        "roots": (4, 4, 2, 2),
        "g_send": (2, 4, 1, 2),
        "g_mid": (2, 1, 4, 2),
        "g_relay2": (2, 2, 1, 2),
        "mats": (3, 4, 4, 2, 2),
        "owned_parcels": (2, 4, 4, 2),
        "owned_middle": (2, 4, 4, 2),
        "owned_relay": (2, 2, 2, 2, 2),
        "hold": (3, 12, 2),
        "z_far": (2, 6, 2),
        "z_plain": (2, 6, 2),
        "z_merged": (2, 6, 2),
        "root_send": (2, 4, 2, 2),
        "root_mid": (2, 2, 4, 2),
        "r_relay2": (2, 2, 2, 2),
        "result": (4, 4, 2),
        "back": (2, 2, 4),
        "home": (2, 4, 2),
        "update": (3, 2, 2),
        "u_relay": (2, 2, 2),
    }
    scratch = {name: pltpu.VMEM(shape + tile, bf16) for name, shape in vmem.items()}
    scratch["g_relay"] = pltpu.VMEM((2, 2, 1, 2, 16, tile[1] // 2), bf16)
    scratch["r_relay"] = pltpu.VMEM((2, 2, 2, 2, 16, tile[1] // 2), bf16)
    scratch["u_relay2"] = pltpu.VMEM((2, 2, 2, 16, tile[1] // 2), bf16)
    scratch["mixed"] = pltpu.VMEM((512, tile[1]), bf16)
    scratch["blocks"] = pltpu.SMEM((32,), jnp.int32)
    scratch["send"] = pltpu.SemaphoreType.DMA((256,))
    scratch["recv"] = pltpu.SemaphoreType.DMA((256,))
    names = ["parts", "owners", "root", "results"] + list(scratch)
    anywhere = pl.BlockSpec(memory_space=pl.ANY)
    return pl.pallas_call(
        functools.partial(step_kernel, names),
        out_shape=jax.ShapeDtypeStruct((RESULTS, 4, 2, 2) + tile, bf16),
        in_specs=[anywhere, pl.BlockSpec(memory_space=pltpu.SMEM), anywhere],
        out_specs=anywhere,
        scratch_shapes=list(scratch.values()),
        compiler_params=pltpu.CompilerParams(
            collective_id=0, has_side_effects=True, vmem_limit_bytes=58 * 2**20
        ),
    )(grads.reshape((6, 4, 4, 2, 2) + tile), owner_slots, root.reshape((4, 4, 2, 2) + tile))


def stats_kernel(owners, results, old_ref, new_ref, update_out, block, turned, stats, held, sem):
    me = lax.axis_index("dp") * 4 + lax.axis_index("tensor")
    parts = [pl.ds(256 * i, 256) for i in range(4)]
    copy = pltpu.make_async_copy
    fetches = [copy(results.at[i], block.at[i], sem.at[i]) for i in range(4)]
    loads = [copy(old_ref.at[parts[i]], stats.at[parts[i]], sem.at[4 + i]) for i in range(4)]
    stores = [copy(stats.at[parts[i]], new_ref.at[parts[i]], sem.at[8 + i]) for i in range(4)]
    take, give = copy(results.at[4, pl.ds(0, 3)], held, sem.at[12]), copy(held, update_out, sem.at[13])
    for each in fetches + [take] + loads:
        each.start()
    is_left, is_right = owners[0, 0] == me, owners[1, 0] == me
    for b in range(1, 24):
        is_left = jnp.logical_or(is_left, owners[0, b] == me)
        is_right = jnp.logical_or(is_right, owners[1, b] == me)
    named = jnp.logical_or(is_left, is_right)

    def rows(i):
        return block[i].reshape(256, 1024)

    def turn(i):
        turned[:, parts[i]] = rows(i).T

    for i in range(4):
        fetches[i].wait()
        pl.when(named)(functools.partial(turn, i))
    take.wait()
    give.start()

    def blend(i, some, other):
        gram = jnp.dot(some, other, preferred_element_type=f32)
        stats[parts[i], :] = decay_rate * stats[parts[i], :] + (1 - decay_rate) * (gram * 1024 ** (-0.5))

    for i in range(4):
        loads[i].wait()
        pl.when(is_left)(lambda i=i: blend(i, rows(i), turned[...]))
        pl.when(is_right)(lambda i=i: blend(i, turned[parts[i], :], block[...].reshape(1024, 1024)))
        stores[i].start()
    for each in stores + [give]:
        each.wait()


def finish_stats(owner_slots, results, old):
    anywhere = pl.BlockSpec(memory_space=pl.ANY)
    tile = results.shape[-2:]
    return pl.pallas_call(
        stats_kernel,
        out_shape=(
            jax.ShapeDtypeStruct(old.shape, f32),
            jax.ShapeDtypeStruct((3, 2, 2) + tile, bf16),
        ),
        in_specs=[pl.BlockSpec(memory_space=pltpu.SMEM), anywhere, anywhere],
        out_specs=(anywhere, anywhere),
        scratch_shapes=[
            pltpu.VMEM((4, 4, 2, 2) + tile, bf16),
            pltpu.VMEM((1024, 1024), bf16),
            pltpu.VMEM(old.shape, f32),
            pltpu.VMEM((3, 2, 2) + tile, bf16),
            pltpu.SemaphoreType.DMA((14,)),
        ],
        compiler_params=pltpu.CompilerParams(vmem_limit_bytes=40 * 2**20),
    )(owner_slots, results, old)


def body(partial_grads, owner_slots, statistics, inv_roots):
    owners = owner_slots.T
    results = step(partial_grads[0], owners, inv_roots[0, 0, 0])
    new_stats, update = finish_stats(owners, results, statistics[0, 0, 0])
    return (new_stats[None, None, None], update.reshape(6, 32, 1024))


def solution(mesh):
    return jax.shard_map(
        body,
        mesh=mesh,
        in_specs=(
            P("dp", "tensor", None, None),
            P(),
            P("dp", "tensor", None, None, None),
            P("dp", "tensor", None, None, None),
        ),
        out_specs=(P("dp", "tensor", None, None, None), P("tensor", "dp", None)),
        check_vma=False,
    )
```

```python
import functools

import jax
import jax.numpy as jnp
from jax import lax
from jax.experimental import pallas as pl
from jax.experimental.pallas import tpu as pltpu
from jax.sharding import PartitionSpec as P

decay_rate = 0.9
MESH = pl.DeviceIdType.MESH
f32 = jnp.float32
bf16 = jnp.bfloat16
lo, hi = pl.ds(0, 3), pl.ds(3, 3)


def place():
    d = lax.axis_index("dp")
    return lax.div(d, 8), lax.rem(lax.div(d, 2), 4), lax.rem(d, 2), lax.axis_index("tensor")


def wrap(v):
    return lax.rem(v + 8, 4)


def remote(src, dst, send, recv, device):
    return pltpu.make_async_remote_copy(
        src_ref=src, dst_ref=dst, send_sem=send, recv_sem=recv, device_id=device, device_id_type=MESH
    )


class Net:
    def __init__(self, send, recv):
        self.x, self.y, self.c, self.t = place()
        self.send, self.recv, self.count, self.open = send, recv, 0, []
        self.at = {"x": self.x, "y": self.y, "z": self.t}
        self.pair = ((self.x * 4 + self.y) * 2 + 1 - self.c, self.t)

    def near(self, axis, step, swap=0):
        x, y, t = [wrap(self.at[a] + step) if a == axis else self.at[a] for a in "xyz"]
        return ((x * 4 + y) * 2 + (1 - self.c if swap else self.c), t)

    def greet(self):
        barrier = pltpu.get_barrier_semaphore()
        peers = [self.pair] + [self.near(axis, step) for axis in "xyz" for step in (1, -1)]
        peers += [self.near(axis, step, 1) for axis in "xy" for step in (1, -1)]
        for peer in peers:
            pl.semaphore_signal(barrier, inc=1, device_id=peer, device_id_type=MESH)
        pl.semaphore_wait(barrier, len(peers))

    def make(self, src, dst, device):
        copy = remote(src, dst, self.send.at[self.count], self.recv.at[self.count], device)
        self.count += 1
        return copy

    def start(self, src, dst, device, when=None):
        copy = self.make(src, dst, device)
        if when is None:
            copy.start()
        else:
            pl.when(when)(copy.start)
        self.open.append((copy, when))
        return copy

    def fork(self, two, ends, device):
        copies = []
        for count, when in ((2, two), (1, jnp.logical_not(two))):
            src, dst = ends(pl.ds(0, count))
            copies.append(self.start(src, dst, device, when))
        return copies

    def join(self, two, copies):
        pl.when(two)(copies[0].wait_recv)
        pl.when(jnp.logical_not(two))(copies[1].wait_recv)

    def local(self, src, dst):
        copy = pltpu.make_async_copy(src, dst, self.send.at[self.count])
        self.count += 1
        copy.start()
        return copy

    def close(self, count):
        for copy, when in self.open[:count]:
            if when is None:
                copy.wait_send()
            else:
                pl.when(when)(copy.wait_send)
        self.open = self.open[count:]


class Exchange:
    def __init__(self, net, axis, src, dst, relay):
        self.net, self.axis, self.dst, self.relay = net, axis, dst, relay
        here = net.at[axis]
        self.i = [wrap(here + o) for o in range(4)]
        right, left = net.near(axis, 1), net.near(axis, -1)
        self.far = [
            net.start(src(self.i[2], 0), relay.at[0], right),
            net.start(src(self.i[2], 1), relay.at[1], left),
        ]
        self.own = net.local(src(self.i[0], None), dst(self.i[0], None))
        self.direct = [
            net.start(src(self.i[1], None), dst(self.i[0], None), right),
            net.start(src(self.i[3], None), dst(self.i[0], None), left),
        ]

        self.passed = []

    def forward(self, way):
        self.far[way].wait_recv()
        source = self.i[3 if way == 0 else 1]
        self.passed.append(
            self.net.start(self.relay.at[way], self.dst(source, way), self.net.near(self.axis, 1 - 2 * way))
        )

    def finish(self):
        self.own.wait()
        for copy in self.direct + self.passed:
            copy.wait_recv()


def half(h):
    return slice(None) if h is None else pl.ds(2 * h, 2)


class LastLeg:
    def __init__(self, net, axis, src, dst, relay):
        self.net, self.axis, self.dst, self.relay = net, axis, dst, relay
        here = net.at[axis]
        self.i = [wrap(here + o) for o in range(4)]
        self.cores = [net.c, 1 - net.c]
        every = slice(None)
        self.far = [
            net.start(src(self.i[2], way, every), relay.at[way], net.near(axis, 1 - 2 * way)) for way in range(2)
        ]
        self.arrive = [
            net.start(src(self.i[o], None, self.cores[k]), dst(self.i[0], None), net.near(axis, step, k))
            for o, step in ((1, 1), (3, -1))
            for k in range(2)
        ]
        self.own = net.local(src(self.i[0], None, self.cores[0]), dst(self.i[0], None))
        self.arrive.append(net.start(src(self.i[0], None, self.cores[1]), dst(self.i[0], None), net.pair))

    def forward(self, way):
        net = self.net
        source = self.i[3 if way == 0 else 1]
        self.far[way].wait_recv()
        self.arrive += [
            net.start(
                self.relay.at[way, :, self.cores[k]], self.dst(source, way), net.near(self.axis, 1 - 2 * way, k)
            )
            for k in range(2)
        ]

    def finish(self):
        self.own.wait()
        for copy in self.arrive:
            copy.wait_recv()


class PlaneExchange:
    def __init__(self, net, parcels, middle, landing, relay):
        self.net, self.parcels, self.middle, self.landing, self.relay = net, parcels, middle, landing, relay
        self.legs = {}

    def first(self, s):
        a, d = self.parcels, self.middle

        def parcels(i, h):
            return a(0, i, half(h)) if s == 0 else a(1, half(h), i)

        self.legs[0, s] = Exchange(
            self.net, "xy"[s], parcels, lambda i, h: d.at[s, i, half(h)], self.relay.at[0, s]
        )

    def second(self, s):
        d, z, c = self.middle, self.landing, self.net.c
        self.legs[0, s].finish()

        def land(j, h):
            return z.at[half(h), j, c, 0] if s == 0 else z.at[j, half(h), c, 1]

        self.legs[1, s] = LastLeg(
            self.net, "yx"[s], lambda j, h, k: d.at[s, half(h), j, k], land, self.relay.at[1, s]
        )

    def finish(self):
        for s in range(2):
            self.legs[1, s].finish()


class WorkerLeg:
    def __init__(self, net, s, source, target, relay):
        self.net, self.axis, self.target, self.relay = net, "xy"[s], target, relay
        here = net.at[self.axis]
        self.i = i = [wrap(here + o) for o in range(4)]
        self.two = [v < 2 if s == 0 else v >= 2 for v in i]
        wide = relay.shape[-1]
        self.cols = [pl.ds(0, wide), pl.ds(wide, wide)]
        self.far = [
            net.fork(
                self.two[2],
                lambda ranks: (source.at[i[2], :, ranks, :, self.cols[way]], relay.at[way, :, ranks]),
                net.near(self.axis, 1 - 2 * way),
            )
            for way in range(2)
        ]
        self.arrive = [
            net.fork(
                self.two[o],
                lambda ranks: (source.at[i[o], :, ranks], target.at[:, i[0], ranks]),
                net.near(self.axis, step),
            )
            for o, step in ((1, 1), (3, -1))
        ]
        self.own = net.local(source.at[i[0]], target.at[:, i[0]])

    def forward(self, way):
        o, goal = ((3, 1), (1, 3))[way]
        self.net.join(self.two[goal], self.far[way])
        self.arrive.append(
            self.net.fork(
                self.two[goal],
                lambda ranks: (
                    self.relay.at[way, :, ranks],
                    self.target.at[:, self.i[o], ranks, :, self.cols[way]],
                ),
                self.net.near(self.axis, 1 - 2 * way),
            )
        )

    def finish(self):
        self.own.wait()
        for copies in self.arrive:
            self.net.join(self.two[0], copies)


class HomeLeg:
    def __init__(self, net, s, back, home, relay):
        self.net, self.axis, self.home, self.relay = net, "xy"[s], home, relay
        here = net.at[self.axis]
        self.i = i = [wrap(here + o) for o in range(4)]
        self.two = [v < 2 if s == 0 else v >= 2 for v in i]
        wide = relay.shape[-1]
        self.cols = [pl.ds(0, wide), pl.ds(wide, wide)]
        self.far = [
            net.fork(
                self.two[0],
                lambda ranks: (back.at[ranks, i[2], :, self.cols[way]], relay.at[way, ranks]),
                net.near(self.axis, 1 - 2 * way),
            )
            for way in range(2)
        ]
        self.direct = [
            net.fork(
                self.two[0],
                lambda ranks: (back.at[ranks, i[o]], home.at[i[0], ranks]),
                net.near(self.axis, step),
            )
            for o, step in ((1, 1), (3, -1))
        ]
        self.own = net.local(back.at[:, i[0]], home.at[i[0]])
        self.passed = []

    def forward(self, way):
        o = (3, 1)[way]
        self.net.join(self.two[o], self.far[way])
        self.passed.append(
            self.net.fork(
                self.two[o],
                lambda ranks: (
                    self.relay.at[way, ranks],
                    self.home.at[self.i[o], ranks, :, self.cols[way]],
                ),
                self.net.near(self.axis, 1 - 2 * way),
            )
        )

    def finish(self):
        self.own.wait()
        for copies, o in zip(self.direct + self.passed, (3, 1, 2, 2)):
            self.net.join(self.two[o], copies)


def spot(s, block):
    if block < 4:
        return block, 0
    return (block - 4, 1) if s == 0 else (block - 2, 1)


class Workers:
    def __init__(self, net):
        self.net = net
        self.is_worker = lax.rem(net.x - net.y + 4, 2) == 0
        self.is_other = lax.rem(net.x - net.y + 4, 2) == 1
        self.ij = [(net.x, net.y), (net.y, net.x)]
        self.axes = ["y", "x"]

    def rank(self, s, step):
        i, j = self.ij[s]
        return lax.div(wrap(j + step - i), 2)

    def beside(self, s):
        return self.net.near(self.axes[s], 1), self.net.near(self.axes[s], -1)


class Gather:
    def __init__(self, w, s, unit, land, relay):
        self.w, net = w, w.net
        right, left = w.beside(s)
        j = [wrap(w.ij[s][1] + o) for o in range(4)]
        self.far = [
            net.make(unit(w.rank(s, 2), 0), relay.at[0], right),
            net.make(unit(w.rank(s, 2), 1), relay.at[1], left),
        ]
        self.direct = [
            net.make(unit(w.rank(s, 1), None), land(j[0], None), right),
            net.make(unit(w.rank(s, 3), None), land(j[0], None), left),
        ]
        self.passed = [
            net.make(relay.at[0], land(j[3], 0), right),
            net.make(relay.at[1], land(j[1], 1), left),
        ]
        self.own = pltpu.make_async_copy(unit(w.rank(s, 0), None), land(j[0], None), net.send.at[net.count])
        net.count += 1

        @pl.when(w.is_worker)
        def _():
            for copy in self.far + [self.own]:
                copy.start()

        @pl.when(w.is_other)
        def _():
            for copy in self.direct:
                copy.start()

        net.open += [(copy, w.is_worker) for copy in self.far]
        net.open += [(copy, w.is_other) for copy in self.direct + self.passed]

    def forward(self):
        @pl.when(self.w.is_other)
        def _():
            for arrived, onward in zip(self.far, self.passed):
                arrived.wait_recv()
                onward.start()

    def wait_here(self):
        self.own.wait()
        for copy in self.direct + self.passed:
            copy.wait_recv()


class Spread:
    def __init__(self, w, s, unit, land, relay):
        self.w, net = w, w.net
        right, left = w.beside(s)
        j = [wrap(w.ij[s][1] + o) for o in range(4)]
        mine = w.rank(s, 0)
        self.far = [net.make(unit(j[2], 0), relay.at[0], right), net.make(unit(j[2], 1), relay.at[1], left)]
        self.direct = [
            net.make(unit(j[1], None), land(mine, None), right),
            net.make(unit(j[3], None), land(mine, None), left),
        ]
        self.passed = [
            net.make(relay.at[0], land(w.rank(s, 3), 0), right),
            net.make(relay.at[1], land(w.rank(s, 1), 1), left),
        ]
        self.own = pltpu.make_async_copy(unit(j[0], None), land(mine, None), net.send.at[net.count])
        net.count += 1

        @pl.when(w.is_worker)
        def _():
            for copy in self.far + self.direct + [self.own]:
                copy.start()

        net.open += [(copy, w.is_worker) for copy in self.far + self.direct]
        net.open += [(copy, w.is_other) for copy in self.passed]

    def forward(self):
        @pl.when(self.w.is_other)
        def _():
            for arrived, onward in zip(self.far, self.passed):
                arrived.wait_recv()
                onward.start()

    def finish(self):
        @pl.when(self.w.is_other)
        def _():
            for copy in self.direct:
                copy.wait_recv()

        @pl.when(self.w.is_worker)
        def _():
            self.own.wait()
            for copy in self.passed:
                copy.wait_recv()


class ReduceScatter:
    def __init__(self, net, parts, v):
        self.net, self.parts, self.v = net, parts, v
        at = [(net.x, net.y), (net.y, net.x)]
        self.i = [[wrap(at[s][0] + o) for o in range(4)] for s in range(2)]
        self.j = [[wrap(at[s][1] + o) for o in range(4)] for s in range(2)]
        self.loads, self.swaps, self.copies = {}, {}, {}

    def fetch(self, order):
        net, own, cin = self.net, self.v["own"], self.v["cin"]

        def view(s, i, core):
            return self.parts.at[:, i, :, core, 0] if s == 0 else self.parts.at[:, :, i, core, 1]

        for o in order:
            for s in range(2):
                i = self.i[s][o]
                self.swaps[s, o] = net.start(view(s, i, 1 - net.c), cin.at[s, i], net.pair)
                self.loads[s, o] = net.local(view(s, i, net.c), own.at[s, i])

    def ship(self, stage, s, way, src, dst):
        axis = "xy"[s] if stage < 3 else "yx"[s]
        self.copies[stage, s, way] = self.net.start(src, dst, self.net.near(axis, 1 - 2 * way))

    def ready(self, s, o):
        self.loads[s, o].wait()
        self.swaps[s, o].wait_recv()

    def add(self, out, terms, blocks):
        @pl.loop(0, blocks)
        def _(b):
            for j in range(4):
                total = terms[0][b, j].astype(f32)
                for term in terms[1:]:
                    total = total + term[b, j].astype(f32)
                out[b, j] = total.astype(bf16)

    def far(self, s):
        own, cin, first_in = self.v["own"], self.v["cin"], self.v["first_in"]
        i = self.i[s][2]
        self.ready(s, 2)
        self.add(own.at[s, i], [own.at[s, i], cin.at[s, i]], 6)
        self.ship(0, s, 0, own.at[s, i, lo], first_in.at[0, s, 0])
        self.ship(0, s, 1, own.at[s, i, hi], first_in.at[0, s, 1])

    def plain(self, way, s):
        own, cin, first_in = self.v["own"], self.v["cin"], self.v["first_in"]
        o, part = ((1, hi), (3, lo))[way]
        i = self.i[s][o]
        self.ready(s, o)
        self.add(own.at[s, i, part], [own.at[s, i, part], cin.at[s, i, part]], 3)
        self.ship(1, s, way, own.at[s, i, part], first_in.at[1, s, way])

    def merged(self, way, s):
        own, cin, first_in = self.v["own"], self.v["cin"], self.v["first_in"]
        o, part = ((1, lo), (3, hi))[way]
        i = self.i[s][o]
        self.copies[0, s, way].wait_recv()
        terms = [own.at[s, i, part], cin.at[s, i, part], first_in.at[0, s, way]]
        self.add(own.at[s, i, part], terms, 3)
        self.ship(2, s, way, own.at[s, i, part], first_in.at[2, s, way])

    def first_sum(self, s, j, b):
        own, cin, first_in = self.v["own"], self.v["cin"], self.v["first_in"]
        i = self.i[s][0]
        total = own[s, i, b, j].astype(f32) + cin[s, i, b, j].astype(f32)
        k, low = (b, 0) if b < 3 else (b - 3, 1)
        for stage, way in ((2, low), (1, 1 - low)):
            total = total + first_in[stage, s, way, k, j].astype(f32)
        return total

    def second(self, s):
        f, second_in = self.v["f"], self.v["second_in"]
        self.ready(s, 0)
        for stage in (1, 2):
            for way in range(2):
                self.copies[stage, s, way].wait_recv()
        j = self.j[s][2]
        for b in range(6):
            f[s, j, b] = self.first_sum(s, j, b).astype(bf16)
        self.ship(3, s, 0, f.at[s, j, lo], second_in.at[0, s, 0])
        self.ship(3, s, 1, f.at[s, j, hi], second_in.at[0, s, 1])

    def second_plain(self, way, s):
        f, second_in = self.v["f"], self.v["second_in"]
        o, part = ((1, hi), (3, lo))[way]
        j = self.j[s][o]
        for b in range(6):
            f[s, j, b] = self.first_sum(s, j, b).astype(bf16)
        self.ship(4, s, way, f.at[s, j, part], second_in.at[1, s, way])

    def second_merged(self, way, s):
        f, second_in = self.v["f"], self.v["second_in"]
        o, part, start = ((1, lo, 0), (3, hi, 3))[way]
        j = self.j[s][o]
        self.copies[3, s, way].wait_recv()
        for k in range(3):
            total = f[s, j, start + k].astype(f32) + second_in[0, s, way, k].astype(f32)
            f[s, j, start + k] = total.astype(bf16)
        self.ship(5, s, way, f.at[s, j, part], second_in.at[2, s, way])

    def finish(self, s, out):
        second_in = self.v["second_in"]
        for stage in (4, 5):
            for way in range(2):
                self.copies[stage, s, way].wait_recv()
        j = self.j[s][0]
        for b in range(6):
            total = self.first_sum(s, j, b)
            k, low = (b, 0) if b < 3 else (b - 3, 1)
            total = total + second_in[2, s, low, k].astype(f32)
            total = total + second_in[1, s, 1 - low, k].astype(f32)
            out[b, s] = total.astype(bf16)


(
    BLK, FAR, FETCH, G, GG, GGF, GL, GLF, MERGED, MMA, MMB, OW1, OW1F, OW2, OW2F, OWE, PLAIN, RG, RGF, RL, RLF,
    RO1, RO1F, RO2, RO2F, SEC, SECM, SECP, SH0, SH1, SP, SPF, UL, ULE, ULF, ZAF, ZF, ZM, ZP, ZSEL,
) = range(40)
CLOSING = (ULF, 0, 1)
RESULTS = 40
ORDER = (
    (RO1, 1), (RO1, 0), (BLK,), (RO1F, 1, 1), (RO1F, 0, 1), (RO1F, 1, 0), (RO1F, 0, 0), (FETCH,), (RO2, 1),
    (RO2, 0), (RO2F, 0, 0), (RO2F, 1, 1), (RO2F, 1, 0), (FAR, 0), (PLAIN, 0, 0), (RO2F, 0, 1), (FAR, 1), (ZF,),
    (PLAIN, 1, 0), (PLAIN, 0, 1), (PLAIN, 1, 1), (ZP,), (ZM, 1), (MERGED, 0, 1), (MERGED, 1, 0),
    (MERGED, 0, 0), (MERGED, 1, 1), (ZM, 0), (SEC, 0), (SEC, 1), (SECP, 1, 1), (SECP, 0, 0), (SECP, 1, 0),
    (SECP, 0, 1), (ZSEL,), (SECM, 0, 0), (SECM, 1, 0), (SECM, 1, 1), (SECM, 0, 1), (RL, 1), (RL, 0), (G, 0),
    (G, 1), (GL, 0), (RLF, 1, 1), (GL, 1), (RLF, 1, 0), (GLF, 1, 0), (GLF, 0, 0), (RLF, 0, 0), (GLF, 0, 1),
    (GLF, 1, 1), (RLF, 0, 1), (RG, 1), (GG, 0), (GGF, 0), (ZAF, 0, 0), (ZAF, 0, 1), (ZAF, 1, 1), (RG, 0),
    (GG, 1), (GGF, 1), (ZAF, 1, 0), (RGF, 1), (OW1, 0), (RGF, 0), (OW1, 1), (SH0,), (SH1,), (MMA,),
    (OW1F, 0, 0), (OW1F, 0, 1), (OW1F, 1, 0), (OW1F, 1, 1), (MMB,), (SP,), (SPF, 0), (SPF, 1), (OW2, 1),
    (OW2, 0), (UL, 0), (OW2F, 1, 0), (UL, 1), (ULF, 0, 1), (ULF, 1, 0), (ULF, 0, 0), (OW2F, 0, 0), (ULF, 1, 1),
    (OW2F, 1, 1), (OW2F, 0, 1), (ULE,), (OWE,),
)


def step_kernel(names, *refs):
    v = dict(zip(names, refs))
    net = Net(v["send"], v["recv"])
    t, c = net.t, net.c
    owners, g, root, blocks = v["owners"], v["g"], v["root"], v["blocks"]
    every = [v["every_0"], v["every_1"]]
    net.greet()
    right, left = net.near("z", 1), net.near("z", -1)
    plane = [wrap(t + o) for o in range(4)]
    sums = ReduceScatter(net, v["parts"], v)
    workers = Workers(net)
    steps, kept = {}, {}

    def step(name):
        def keep(function):
            steps[name] = function

        return keep

    @step((FETCH,))
    def _():
        sums.fetch((2, 1, 3, 0))

    @step((BLK,))
    def _():
        @pl.loop(0, 32)
        def _(d):
            slot, block = d * 4 + t, jnp.int32(0)
            for b in range(24):
                hit = jnp.logical_or(owners[0, b] == slot, owners[1, b] == slot)
                block = jnp.where(hit, b, block)
            blocks[d] = block

    roots = PlaneExchange(
        net, lambda s, x, y: root.at[x, y, :, s], v["root_middle"], v["roots"], v["root_relay"]
    )
    parcels = v["owned_parcels"]
    owned = PlaneExchange(
        net, lambda s, x, y: parcels.at[s, x, y], v["owned_middle"], v["results"].at[pl.ds(0, 4)], v["owned_relay"]
    )

    def pack_owned(s):
        kept["g_own", s].wait()
        for way in range(2):
            kept["g_pass", s, way].wait_recv()

        @pl.loop(0, 16)
        def _(chip):
            x, y = lax.div(chip, 4), lax.rem(chip, 4)
            for core in range(2):
                block = blocks[2 * chip + core]
                parcels[s, x, y, core] = every[s][lax.div(block, 6), lax.rem(block, 6)]

        owned.first(s)

    pieces, hold = v["roots"], v["hold"]
    far_in, plain_in, merged_in = v["z_far"], v["z_plain"], v["z_merged"]
    first_k, last_k = pl.ds(0, 6), pl.ds(6, 6)

    def wanted(target, k):
        slot = owners[lax.div(k, 6), target * 6 + lax.rem(k, 6)]
        d = lax.div(slot, 4)
        return lax.rem(slot, 4), pieces[lax.div(d, 8), lax.rem(lax.div(d, 2), 4), lax.rem(d, 2)]

    def fill(o, start, arrived=None):
        @pl.loop(0, 6)
        def _(n):
            where, rows = wanted(plane[o], start + n)
            if arrived is not None:
                rows = lax.select(where == t, rows, arrived[n])
            hold[o - 1, start + n] = rows

    @step((ZF,))
    def _():
        roots.finish()
        fill(2, 0)
        fill(2, 6)
        kept["z", 0] = [
            net.start(hold.at[1, first_k], far_in.at[0], right),
            net.start(hold.at[1, last_k], far_in.at[1], left),
        ]

    @step((ZP,))
    def _():
        fill(1, 6)
        fill(3, 0)
        kept["z", 1] = [
            net.start(hold.at[0, last_k], plain_in.at[0], right),
            net.start(hold.at[2, first_k], plain_in.at[1], left),
        ]

    @step((ZM, 0))
    def _():
        kept["z", 0][0].wait_recv()
        fill(1, 0, far_in.at[0])
        kept["z", 2] = net.start(hold.at[0, first_k], merged_in.at[0], right)

    @step((ZM, 1))
    def _():
        kept["z", 0][1].wait_recv()
        fill(3, 6, far_in.at[1])
        kept["z", 3] = net.start(hold.at[2, last_k], merged_in.at[1], left)

    root_send, root_mid = v["root_send"], v["root_mid"]

    @step((ZSEL,))
    def _():
        for copy in kept["z", 1] + [kept["z", 2], kept["z", 3]]:
            copy.wait_recv()
        for side in range(2):
            for block in range(6):
                where, rows = wanted(t, side * 6 + block)
                away = wrap(where - t)
                if side == 0:
                    other_rows = lax.select(away == 1, plain_in[1, block], merged_in[0, block])
                else:
                    other_rows = lax.select(away == 3, plain_in[0, block], merged_in[1, block])
                rows = lax.select(away == 0, rows, other_rows)
                for s in range(2):
                    line, rank = spot(s, block)
                    root_send[s, line, side, rank] = rows[s]

    g_send, g_mid = v["g_send"], v["g_mid"]

    def sum_up(s):
        sums.finish(s, g)
        here, there = g.at[:, s], every[s].at[t]
        kept["g", s] = [net.start(here, there, right), net.start(here, there, left)]
        kept["g_own", s] = net.local(here, there)

    def pass_along(s, way):
        kept["g", s][way].wait_recv()
        rows = every[s].at[plane[3], lo] if way == 0 else every[s].at[plane[1], hi]
        kept["g_pass", s, way] = net.start(rows, rows, right if way == 0 else left)

    def send_g(s):
        for block in range(6):
            line, rank = spot(s, block)
            g_send[s, line, 0, rank] = g[block, s]
        kept["gl", s] = WorkerLeg(net, s, g_send.at[s], g_mid.at[s], v["g_relay"].at[s])

    def send_roots(s):
        kept["rl", s] = WorkerLeg(net, s, root_send.at[s], root_mid.at[s], v["r_relay"].at[s])

    mats = v["mats"]

    def gather(name, leg, s, mid, first, count, relay):
        def land(j, h):
            if s == 0:
                return mats.at[pl.ds(first, count), half(h), j, c, 0]
            return mats.at[pl.ds(first, count), j, half(h), c, 1]

        kept[leg, s].finish()
        kept[name, s] = Gather(workers, s, lambda rank, h: mid.at[s, :, half(h), rank], land, relay.at[s])

    shares = [net.make(mats.at[m, :, :, c], mats.at[m, :, :, c], net.pair) for m in (2, 1)]
    net.open += [(copy, workers.is_worker) for copy in shares]
    mixed, result = v["mixed"], v["result"]

    def share(name, k):
        @pl.when(workers.is_worker)
        def _():
            for s in range(2):
                kept[name, s].wait_here()
            shares[k].start()

    def column_tiles(function):
        @pl.loop(0, 4)
        def _(n):
            function(pl.ds(pl.multiple_of(n * 256, 256), 256))

    @step((MMA,))
    def _():
        @pl.when(workers.is_worker)
        def _():
            shares[0].wait_recv()

            @column_tiles
            def _(cols):
                block = mats[2, :, :, :, :, :, cols].reshape(1024, 256)
                rows = mats[0, :, :, c].reshape(512, 1024)
                mixed[:, cols] = jnp.dot(rows, block, preferred_element_type=f32).astype(bf16)

    @step((MMB,))
    def _():
        @pl.when(workers.is_worker)
        def _():
            shares[1].wait_recv()

            @column_tiles
            def _(cols):
                block = mats[1, :, :, :, :, :, cols].reshape(1024, 256)
                rows = jnp.dot(mixed[...], block, preferred_element_type=f32).astype(bf16)
                result[:, :, :, :, cols] = rows.reshape(4, 4, 2, 16, 256)

    back, home = v["back"], v["home"]

    @step((SP,))
    def _():
        for s in range(2):
            kept["sp", s] = Spread(
                workers,
                s,
                lambda j, h, s=s: result.at[half(h), j, 0] if s == 0 else result.at[j, half(h), 1],
                lambda rank, h, s=s: back.at[s, rank, half(h)],
                v["u_relay"].at[s],
            )

    def go_home(s):
        kept["sp", s].finish()
        kept["ul", s] = HomeLeg(net, s, back.at[s], home.at[s], v["u_relay2"].at[s])

    @step((ULE,))
    def _():
        for s in range(2):
            kept["ul", s].finish()
            for block in range(6):
                line, rank = spot(s, block)
                v["update"][block // 2, block % 2, s] = home[s, line, rank]
        kept["update"] = net.local(v["update"], v["results"].at[4, pl.ds(0, 3)])

    steps[(OWE,)] = owned.finish
    steps[(SH0,)] = functools.partial(share, "gg", 0)
    steps[(SH1,)] = functools.partial(share, "rg", 1)
    for s in range(2):
        bind = functools.partial
        steps[RO1, s] = bind(roots.first, s)
        steps[RO2, s] = bind(roots.second, s)
        steps[OW1, s] = bind(pack_owned, s)
        steps[OW2, s] = bind(owned.second, s)
        steps[FAR, s] = bind(sums.far, s)
        steps[SEC, s] = bind(sums.second, s)
        steps[G, s] = bind(sum_up, s)
        steps[GL, s] = bind(send_g, s)
        steps[RL, s] = bind(send_roots, s)
        steps[GG, s] = bind(gather, "gg", "gl", s, g_mid, 2, 1, v["g_relay2"])
        steps[RG, s] = bind(gather, "rg", "rl", s, root_mid, 0, 2, v["r_relay2"])
        steps[GGF, s] = lambda s=s: kept["gg", s].forward()
        steps[RGF, s] = lambda s=s: kept["rg", s].forward()
        steps[SPF, s] = lambda s=s: kept["sp", s].forward()
        steps[UL, s] = bind(go_home, s)
        for way in range(2):
            steps[PLAIN, way, s] = bind(sums.plain, way, s)
            steps[MERGED, way, s] = bind(sums.merged, way, s)
            steps[SECP, way, s] = bind(sums.second_plain, way, s)
            steps[SECM, way, s] = bind(sums.second_merged, way, s)
            steps[ZAF, s, way] = bind(pass_along, s, way)
            for name, trip, leg in ((RO1F, roots, 0), (RO2F, roots, 1), (OW1F, owned, 0), (OW2F, owned, 1)):
                steps[name, s, way] = (
                    lambda trip=trip, leg=leg, s=s, way=way: trip.legs[leg, s].forward(way)
                )
            for name, leg in ((GLF, "gl"), (RLF, "rl"), (ULF, "ul")):
                steps[name, s, way] = lambda leg=leg, s=s, way=way: kept[leg, s].forward(way)
    assert sorted(steps) == sorted(ORDER)
    for name in ORDER:
        if name == (MMA,):
            early = len(net.open)
        if name == CLOSING:
            net.close(early)
        steps[name]()
    kept["update"].wait()
    net.close(len(net.open))


def step(grads, owner_slots, root):
    tile = (16, root.shape[1])
    vmem = {
        "own": (2, 4, 6, 4),
        "cin": (2, 4, 6, 4),
        "first_in": (3, 2, 2, 3, 4),
        "f": (2, 4, 6),
        "second_in": (3, 2, 2, 3),
        "g": (6, 2),
        "every_0": (4, 6),
        "every_1": (4, 6),
        "root_middle": (2, 4, 4, 2),
        "root_relay": (2, 2, 2, 2, 2),
        "roots": (4, 4, 2, 2),
        "g_send": (2, 4, 1, 2),
        "g_mid": (2, 1, 4, 2),
        "g_relay2": (2, 2, 1, 2),
        "mats": (3, 4, 4, 2, 2),
        "owned_parcels": (2, 4, 4, 2),
        "owned_middle": (2, 4, 4, 2),
        "owned_relay": (2, 2, 2, 2, 2),
        "hold": (3, 12, 2),
        "z_far": (2, 6, 2),
        "z_plain": (2, 6, 2),
        "z_merged": (2, 6, 2),
        "root_send": (2, 4, 2, 2),
        "root_mid": (2, 2, 4, 2),
        "r_relay2": (2, 2, 2, 2),
        "result": (4, 4, 2),
        "back": (2, 2, 4),
        "home": (2, 4, 2),
        "update": (3, 2, 2),
        "u_relay": (2, 2, 2),
    }
    scratch = {name: pltpu.VMEM(shape + tile, bf16) for name, shape in vmem.items()}
    scratch["g_relay"] = pltpu.VMEM((2, 2, 1, 2, 16, tile[1] // 2), bf16)
    scratch["r_relay"] = pltpu.VMEM((2, 2, 2, 2, 16, tile[1] // 2), bf16)
    scratch["u_relay2"] = pltpu.VMEM((2, 2, 2, 16, tile[1] // 2), bf16)
    scratch["mixed"] = pltpu.VMEM((512, tile[1]), bf16)
    scratch["blocks"] = pltpu.SMEM((32,), jnp.int32)
    scratch["send"] = pltpu.SemaphoreType.DMA((256,))
    scratch["recv"] = pltpu.SemaphoreType.DMA((256,))
    names = ["parts", "owners", "root", "results"] + list(scratch)
    anywhere = pl.BlockSpec(memory_space=pl.ANY)
    return pl.pallas_call(
        functools.partial(step_kernel, names),
        out_shape=jax.ShapeDtypeStruct((RESULTS, 4, 2, 2) + tile, bf16),
        in_specs=[anywhere, pl.BlockSpec(memory_space=pltpu.SMEM), anywhere],
        out_specs=anywhere,
        scratch_shapes=list(scratch.values()),
        compiler_params=pltpu.CompilerParams(
            collective_id=0, has_side_effects=True, vmem_limit_bytes=58 * 2**20
        ),
    )(grads.reshape((6, 4, 4, 2, 2) + tile), owner_slots, root.reshape((4, 4, 2, 2) + tile))


def stats_kernel(owners, results, old_ref, new_ref, update_out, block, turned, stats, held, sem):
    me = lax.axis_index("dp") * 4 + lax.axis_index("tensor")
    parts = [pl.ds(256 * i, 256) for i in range(4)]
    copy = pltpu.make_async_copy
    fetches = [copy(results.at[i], block.at[i], sem.at[i]) for i in range(4)]
    loads = [copy(old_ref.at[parts[i]], stats.at[parts[i]], sem.at[4 + i]) for i in range(4)]
    stores = [copy(stats.at[parts[i]], new_ref.at[parts[i]], sem.at[8 + i]) for i in range(4)]
    take, give = copy(results.at[4, pl.ds(0, 3)], held, sem.at[12]), copy(held, update_out, sem.at[13])
    for each in fetches + [take] + loads:
        each.start()
    is_left, is_right = owners[0, 0] == me, owners[1, 0] == me
    for b in range(1, 24):
        is_left = jnp.logical_or(is_left, owners[0, b] == me)
        is_right = jnp.logical_or(is_right, owners[1, b] == me)
    named = jnp.logical_or(is_left, is_right)

    def rows(i):
        return block[i].reshape(256, 1024)

    def turn(i):
        turned[:, parts[i]] = rows(i).T

    for i in range(4):
        fetches[i].wait()
        pl.when(named)(functools.partial(turn, i))
    take.wait()
    give.start()

    def blend(i, some, other):
        gram = jnp.dot(some, other, preferred_element_type=f32)
        stats[parts[i], :] = decay_rate * stats[parts[i], :] + (1 - decay_rate) * (gram * 1024 ** (-0.5))

    for i in range(4):
        loads[i].wait()
        pl.when(is_left)(lambda i=i: blend(i, rows(i), turned[...]))
        pl.when(is_right)(lambda i=i: blend(i, turned[parts[i], :], block[...].reshape(1024, 1024)))
        stores[i].start()
    for each in stores + [give]:
        each.wait()


def finish_stats(owner_slots, results, old):
    anywhere = pl.BlockSpec(memory_space=pl.ANY)
    tile = results.shape[-2:]
    return pl.pallas_call(
        stats_kernel,
        out_shape=(
            jax.ShapeDtypeStruct(old.shape, f32),
            jax.ShapeDtypeStruct((3, 2, 2) + tile, bf16),
        ),
        in_specs=[pl.BlockSpec(memory_space=pltpu.SMEM), anywhere, anywhere],
        out_specs=(anywhere, anywhere),
        scratch_shapes=[
            pltpu.VMEM((4, 4, 2, 2) + tile, bf16),
            pltpu.VMEM((1024, 1024), bf16),
            pltpu.VMEM(old.shape, f32),
            pltpu.VMEM((3, 2, 2) + tile, bf16),
            pltpu.SemaphoreType.DMA((14,)),
        ],
        compiler_params=pltpu.CompilerParams(vmem_limit_bytes=40 * 2**20),
    )(owner_slots, results, old)


def body(partial_grads, owner_slots, statistics, inv_roots):
    owners = owner_slots.T
    results = step(partial_grads[0], owners, inv_roots[0, 0, 0])
    new_stats, update = finish_stats(owners, results, statistics[0, 0, 0])
    return (new_stats[None, None, None], update.reshape(6, 32, 1024))


def solution(mesh):
    return jax.shard_map(
        body,
        mesh=mesh,
        in_specs=(
            P("dp", "tensor", None, None),
            P(),
            P("dp", "tensor", None, None, None),
            P("dp", "tensor", None, None, None),
        ),
        out_specs=(P("dp", "tensor", None, None, None), P("tensor", "dp", None)),
        check_vma=False,
    )
```

```python
import functools

import jax
import jax.numpy as jnp
from jax import lax
from jax.experimental import pallas as pl
from jax.experimental.pallas import tpu as pltpu
from jax.sharding import PartitionSpec as P

decay_rate = 0.9
MESH = pl.DeviceIdType.MESH
f32 = jnp.float32
bf16 = jnp.bfloat16
lo, hi = pl.ds(0, 3), pl.ds(3, 3)


def place():
    d = lax.axis_index("dp")
    return lax.div(d, 8), lax.rem(lax.div(d, 2), 4), lax.rem(d, 2), lax.axis_index("tensor")


def wrap(v):
    return lax.rem(v + 8, 4)


def remote(src, dst, send, recv, device):
    return pltpu.make_async_remote_copy(
        src_ref=src, dst_ref=dst, send_sem=send, recv_sem=recv, device_id=device, device_id_type=MESH
    )


class Net:
    def __init__(self, send, recv):
        self.x, self.y, self.c, self.t = place()
        self.send, self.recv, self.count, self.open = send, recv, 0, []
        self.at = {"x": self.x, "y": self.y, "z": self.t}
        self.pair = ((self.x * 4 + self.y) * 2 + 1 - self.c, self.t)

    def near(self, axis, step, swap=0):
        x, y, t = [wrap(self.at[a] + step) if a == axis else self.at[a] for a in "xyz"]
        return ((x * 4 + y) * 2 + (1 - self.c if swap else self.c), t)

    def greet(self):
        barrier = pltpu.get_barrier_semaphore()
        peers = [self.pair] + [self.near(axis, step) for axis in "xyz" for step in (1, -1)]
        peers += [self.near(axis, step, 1) for axis in "xy" for step in (1, -1)]
        for peer in peers:
            pl.semaphore_signal(barrier, inc=1, device_id=peer, device_id_type=MESH)
        pl.semaphore_wait(barrier, len(peers))

    def make(self, src, dst, device):
        copy = remote(src, dst, self.send.at[self.count], self.recv.at[self.count], device)
        self.count += 1
        return copy

    def start(self, src, dst, device, when=None):
        copy = self.make(src, dst, device)
        if when is None:
            copy.start()
        else:
            pl.when(when)(copy.start)
        self.open.append((copy, when))
        return copy

    def local(self, src, dst):
        copy = pltpu.make_async_copy(src, dst, self.send.at[self.count])
        self.count += 1
        copy.start()
        return copy

    def close(self, count):
        for copy, when in self.open[:count]:
            if when is None:
                copy.wait_send()
            else:
                pl.when(when)(copy.wait_send)
        self.open = self.open[count:]


class Exchange:
    def __init__(self, net, axis, src, dst, relay):
        self.net, self.axis, self.dst, self.relay = net, axis, dst, relay
        here = net.at[axis]
        self.i = [wrap(here + o) for o in range(4)]
        right, left = net.near(axis, 1), net.near(axis, -1)
        self.far = [
            net.start(src(self.i[2], 0), relay.at[0], right),
            net.start(src(self.i[2], 1), relay.at[1], left),
        ]
        self.own = net.local(src(self.i[0], None), dst(self.i[0], None))
        self.direct = [
            net.start(src(self.i[1], None), dst(self.i[0], None), right),
            net.start(src(self.i[3], None), dst(self.i[0], None), left),
        ]

        self.passed = []

    def forward(self, way):
        self.far[way].wait_recv()
        source = self.i[3 if way == 0 else 1]
        self.passed.append(
            self.net.start(self.relay.at[way], self.dst(source, way), self.net.near(self.axis, 1 - 2 * way))
        )

    def finish(self):
        self.own.wait()
        for copy in self.direct + self.passed:
            copy.wait_recv()


def half(h):
    return slice(None) if h is None else pl.ds(2 * h, 2)


class LastLeg:
    def __init__(self, net, axis, src, dst, relay):
        self.net, self.axis, self.dst, self.relay = net, axis, dst, relay
        here = net.at[axis]
        self.i = [wrap(here + o) for o in range(4)]
        self.cores = [net.c, 1 - net.c]
        every = slice(None)
        self.far = [
            net.start(src(self.i[2], way, every), relay.at[way], net.near(axis, 1 - 2 * way)) for way in range(2)
        ]
        self.arrive = [
            net.start(src(self.i[o], None, self.cores[k]), dst(self.i[0], None), net.near(axis, step, k))
            for o, step in ((1, 1), (3, -1))
            for k in range(2)
        ]
        self.own = net.local(src(self.i[0], None, self.cores[0]), dst(self.i[0], None))
        self.arrive.append(net.start(src(self.i[0], None, self.cores[1]), dst(self.i[0], None), net.pair))

    def forward(self, way):
        net = self.net
        source = self.i[3 if way == 0 else 1]
        self.far[way].wait_recv()
        self.arrive += [
            net.start(
                self.relay.at[way, :, self.cores[k]], self.dst(source, way), net.near(self.axis, 1 - 2 * way, k)
            )
            for k in range(2)
        ]

    def finish(self):
        self.own.wait()
        for copy in self.arrive:
            copy.wait_recv()


class PlaneExchange:
    def __init__(self, net, parcels, middle, landing, relay):
        self.net, self.parcels, self.middle, self.landing, self.relay = net, parcels, middle, landing, relay
        self.legs = {}

    def first(self, s):
        a, d = self.parcels, self.middle

        def parcels(i, h):
            return a(0, i, half(h)) if s == 0 else a(1, half(h), i)

        self.legs[0, s] = Exchange(
            self.net, "xy"[s], parcels, lambda i, h: d.at[s, i, half(h)], self.relay.at[0, s]
        )

    def second(self, s):
        d, z, c = self.middle, self.landing, self.net.c
        self.legs[0, s].finish()

        def land(j, h):
            return z.at[half(h), j, c, 0] if s == 0 else z.at[j, half(h), c, 1]

        self.legs[1, s] = LastLeg(
            self.net, "yx"[s], lambda j, h, k: d.at[s, half(h), j, k], land, self.relay.at[1, s]
        )

    def finish(self):
        for s in range(2):
            self.legs[1, s].finish()


class WorkerLeg:
    def __init__(self, net, s, source, target, relay):
        self.net, self.s, self.axis = net, s, "xy"[s]
        here = net.at[self.axis]
        self.target, self.relay = target, relay
        self.i = i = [wrap(here + o) for o in range(4)]
        self.two = [v < 2 if s == 0 else v >= 2 for v in i]
        wide = relay.shape[-1]
        self.cols = [pl.ds(0, wide), pl.ds(wide, wide)]

        def when(o, rank):
            return self.two[o] if rank else None

        self.when = when
        self.far = [
            [
                net.start(
                    source.at[i[2], :, rank, :, self.cols[way]],
                    relay.at[way, :, rank],
                    net.near(self.axis, 1 - 2 * way),
                    when(2, rank),
                )
                for way in range(2)
            ]
            for rank in range(2)
        ]
        self.direct = [
            [
                net.start(
                    source.at[i[o], :, rank], target.at[:, i[0], rank], net.near(self.axis, step), when(o, rank)
                )
                for o, step in ((1, 1), (3, -1))
            ]
            for rank in range(2)
        ]
        self.own = net.local(source.at[i[0]], target.at[:, i[0]])
        self.passed = [[], []]

    def forward(self, way):
        o, goal = ((3, 1), (1, 3))[way]
        for rank in range(2):
            arrived = self.far[rank][way]
            when = self.when(goal, rank)
            if when is None:
                arrived.wait_recv()
            else:
                pl.when(when)(arrived.wait_recv)
            self.passed[rank].append(
                self.net.start(
                    self.relay.at[way, :, rank],
                    self.target.at[:, self.i[o], rank, :, self.cols[way]],
                    self.net.near(self.axis, 1 - 2 * way),
                    when,
                )
            )

    def finish(self):
        self.own.wait()
        for copy in self.direct[0] + self.passed[0]:
            copy.wait_recv()

        @pl.when(self.two[0])
        def _():
            for copy in self.direct[1] + self.passed[1]:
                copy.wait_recv()


class HomeLeg:
    def __init__(self, net, s, back, home, relay):
        self.net, self.axis, self.home, self.relay = net, "xy"[s], home, relay
        here = net.at[self.axis]
        self.i = i = [wrap(here + o) for o in range(4)]
        self.two = [v < 2 if s == 0 else v >= 2 for v in i]
        wide = relay.shape[-1]
        self.cols = [pl.ds(0, wide), pl.ds(wide, wide)]
        self.far = [
            [
                net.start(
                    back.at[rank, i[2], :, self.cols[way]],
                    relay.at[way, rank],
                    net.near(self.axis, 1 - 2 * way),
                    self.when(0, rank),
                )
                for way in range(2)
            ]
            for rank in range(2)
        ]
        self.direct = [
            [
                net.start(back.at[rank, i[o]], home.at[i[0], rank], net.near(self.axis, step), self.when(0, rank))
                for o, step in ((1, 1), (3, -1))
            ]
            for rank in range(2)
        ]
        self.own = net.local(back.at[:, i[0]], home.at[i[0]])
        self.passed = [[], []]

    def when(self, o, rank):
        return self.two[o] if rank else None

    def arrived(self, copy, o, rank):
        if rank:
            pl.when(self.two[o])(copy.wait_recv)
        else:
            copy.wait_recv()

    def forward(self, way):
        o = (3, 1)[way]
        for rank in range(2):
            self.arrived(self.far[rank][way], o, rank)
            self.passed[rank].append(
                self.net.start(
                    self.relay.at[way, rank],
                    self.home.at[self.i[o], rank, :, self.cols[way]],
                    self.net.near(self.axis, 1 - 2 * way),
                    self.when(o, rank),
                )
            )

    def finish(self):
        self.own.wait()
        for rank in range(2):
            for copy, o in zip(self.direct[rank] + self.passed[rank], (3, 1, 2, 2)):
                self.arrived(copy, o, rank)


def spot(s, block):
    rank = lax.div(block, 4)
    return block - (4, 2)[s] * rank, rank


class Workers:
    def __init__(self, net):
        self.net = net
        self.is_worker = lax.rem(net.x - net.y + 4, 2) == 0
        self.is_other = lax.rem(net.x - net.y + 4, 2) == 1
        self.ij = [(net.x, net.y), (net.y, net.x)]
        self.axes = ["y", "x"]

    def rank(self, s, step):
        i, j = self.ij[s]
        return lax.div(wrap(j + step - i), 2)

    def beside(self, s):
        return self.net.near(self.axes[s], 1), self.net.near(self.axes[s], -1)


class Gather:
    def __init__(self, w, s, unit, land, relay):
        self.w, net = w, w.net
        right, left = w.beside(s)
        j = [wrap(w.ij[s][1] + o) for o in range(4)]
        self.far = [
            net.make(unit(w.rank(s, 2), 0), relay.at[0], right),
            net.make(unit(w.rank(s, 2), 1), relay.at[1], left),
        ]
        self.direct = [
            net.make(unit(w.rank(s, 1), None), land(j[0], None), right),
            net.make(unit(w.rank(s, 3), None), land(j[0], None), left),
        ]
        self.passed = [
            net.make(relay.at[0], land(j[3], 0), right),
            net.make(relay.at[1], land(j[1], 1), left),
        ]
        self.own = pltpu.make_async_copy(unit(w.rank(s, 0), None), land(j[0], None), net.send.at[net.count])
        net.count += 1

        @pl.when(w.is_worker)
        def _():
            for copy in self.far + [self.own]:
                copy.start()

        @pl.when(w.is_other)
        def _():
            for copy in self.direct:
                copy.start()

        net.open += [(copy, w.is_worker) for copy in self.far]
        net.open += [(copy, w.is_other) for copy in self.direct + self.passed]

    def forward(self):
        @pl.when(self.w.is_other)
        def _():
            for arrived, onward in zip(self.far, self.passed):
                arrived.wait_recv()
                onward.start()

    def wait_here(self):
        self.own.wait()
        for copy in self.direct + self.passed:
            copy.wait_recv()


class Spread:
    def __init__(self, w, s, unit, land, relay):
        self.w, net = w, w.net
        right, left = w.beside(s)
        j = [wrap(w.ij[s][1] + o) for o in range(4)]
        mine = w.rank(s, 0)
        self.far = [net.make(unit(j[2], 0), relay.at[0], right), net.make(unit(j[2], 1), relay.at[1], left)]
        self.direct = [
            net.make(unit(j[1], None), land(mine, None), right),
            net.make(unit(j[3], None), land(mine, None), left),
        ]
        self.passed = [
            net.make(relay.at[0], land(w.rank(s, 3), 0), right),
            net.make(relay.at[1], land(w.rank(s, 1), 1), left),
        ]
        self.own = pltpu.make_async_copy(unit(j[0], None), land(mine, None), net.send.at[net.count])
        net.count += 1

        @pl.when(w.is_worker)
        def _():
            for copy in self.far + self.direct + [self.own]:
                copy.start()

        net.open += [(copy, w.is_worker) for copy in self.far + self.direct]
        net.open += [(copy, w.is_other) for copy in self.passed]

    def forward(self):
        @pl.when(self.w.is_other)
        def _():
            for arrived, onward in zip(self.far, self.passed):
                arrived.wait_recv()
                onward.start()

    def finish(self):
        @pl.when(self.w.is_other)
        def _():
            for copy in self.direct:
                copy.wait_recv()

        @pl.when(self.w.is_worker)
        def _():
            self.own.wait()
            for copy in self.passed:
                copy.wait_recv()


class ReduceScatter:
    def __init__(self, net, parts, v):
        self.net, self.parts, self.v = net, parts, v
        at = [(net.x, net.y), (net.y, net.x)]
        self.i = [[wrap(at[s][0] + o) for o in range(4)] for s in range(2)]
        self.j = [[wrap(at[s][1] + o) for o in range(4)] for s in range(2)]
        self.loads, self.swaps, self.copies = {}, {}, {}

    def fetch(self, order):
        net, own, cin = self.net, self.v["own"], self.v["cin"]

        def view(s, i, core):
            return self.parts.at[:, i, :, core, 0] if s == 0 else self.parts.at[:, :, i, core, 1]

        for o in order:
            for s in range(2):
                i = self.i[s][o]
                self.swaps[s, o] = net.start(view(s, i, 1 - net.c), cin.at[s, i], net.pair)
                self.loads[s, o] = net.local(view(s, i, net.c), own.at[s, i])

    def ship(self, stage, s, way, src, dst):
        axis = "xy"[s] if stage < 3 else "yx"[s]
        self.copies[stage, s, way] = self.net.start(src, dst, self.net.near(axis, 1 - 2 * way))

    def ready(self, s, o):
        self.loads[s, o].wait()
        self.swaps[s, o].wait_recv()

    def add(self, out, terms, blocks):
        @pl.loop(0, blocks)
        def _(b):
            for j in range(4):
                total = terms[0][b, j].astype(f32)
                for term in terms[1:]:
                    total = total + term[b, j].astype(f32)
                out[b, j] = total.astype(bf16)

    def far(self, s):
        own, cin, first_in = self.v["own"], self.v["cin"], self.v["first_in"]
        i = self.i[s][2]
        self.ready(s, 2)
        self.add(own.at[s, i], [own.at[s, i], cin.at[s, i]], 6)
        self.ship(0, s, 0, own.at[s, i, lo], first_in.at[0, s, 0])
        self.ship(0, s, 1, own.at[s, i, hi], first_in.at[0, s, 1])

    def plain(self, way, s):
        own, cin, first_in = self.v["own"], self.v["cin"], self.v["first_in"]
        o, part = ((1, hi), (3, lo))[way]
        i = self.i[s][o]
        self.ready(s, o)
        self.add(own.at[s, i, part], [own.at[s, i, part], cin.at[s, i, part]], 3)
        self.ship(1, s, way, own.at[s, i, part], first_in.at[1, s, way])

    def merged(self, way, s):
        own, cin, first_in = self.v["own"], self.v["cin"], self.v["first_in"]
        o, part = ((1, lo), (3, hi))[way]
        i = self.i[s][o]
        self.copies[0, s, way].wait_recv()
        terms = [own.at[s, i, part], cin.at[s, i, part], first_in.at[0, s, way]]
        self.add(own.at[s, i, part], terms, 3)
        self.ship(2, s, way, own.at[s, i, part], first_in.at[2, s, way])

    def first_sum(self, s, j, k, low):
        own, cin, first_in = self.v["own"], self.v["cin"], self.v["first_in"]
        i, b = self.i[s][0], 3 * low + k
        total = own[s, i, b, j].astype(f32) + cin[s, i, b, j].astype(f32)
        total = total + first_in[2, s, low, k, j].astype(f32)
        return total + first_in[1, s, 1 - low, k, j].astype(f32)

    def first_done(self, s, j):
        f = self.v["f"]

        @pl.loop(0, 3)
        def _(k):
            for low in range(2):
                f[s, j, 3 * low + k] = self.first_sum(s, j, k, low).astype(bf16)

    def second(self, s):
        f, second_in = self.v["f"], self.v["second_in"]
        self.ready(s, 0)
        for stage in (1, 2):
            for way in range(2):
                self.copies[stage, s, way].wait_recv()
        j = self.j[s][2]
        self.first_done(s, j)
        self.ship(3, s, 0, f.at[s, j, lo], second_in.at[0, s, 0])
        self.ship(3, s, 1, f.at[s, j, hi], second_in.at[0, s, 1])

    def second_plain(self, way, s):
        f, second_in = self.v["f"], self.v["second_in"]
        o, part = ((1, hi), (3, lo))[way]
        j = self.j[s][o]
        self.first_done(s, j)
        self.ship(4, s, way, f.at[s, j, part], second_in.at[1, s, way])

    def second_merged(self, way, s):
        f, second_in = self.v["f"], self.v["second_in"]
        o, part, start = ((1, lo, 0), (3, hi, 3))[way]
        j = self.j[s][o]
        self.copies[3, s, way].wait_recv()

        @pl.loop(0, 3)
        def _(k):
            total = f[s, j, start + k].astype(f32) + second_in[0, s, way, k].astype(f32)
            f[s, j, start + k] = total.astype(bf16)

        self.ship(5, s, way, f.at[s, j, part], second_in.at[2, s, way])

    def finish(self, s, out):
        second_in = self.v["second_in"]
        for stage in (4, 5):
            for way in range(2):
                self.copies[stage, s, way].wait_recv()
        j = self.j[s][0]

        @pl.loop(0, 3)
        def _(k):
            for low in range(2):
                total = self.first_sum(s, j, k, low)
                total = total + second_in[2, s, low, k].astype(f32)
                total = total + second_in[1, s, 1 - low, k].astype(f32)
                out[3 * low + k, s] = total.astype(bf16)


(
    BLK, FAR, FETCH, G, GG, GGF, GL, GLF, MERGED, MMA, MMB, OW1, OW1F, OW2, OW2F, OWE, PLAIN, RG, RGF, RL, RLF,
    RO1, RO1F, RO2, RO2F, SEC, SECM, SECP, SH0, SH1, SP, SPF, UL, ULE, ULF, ZAF, ZF, ZM, ZP, ZSEL,
) = range(40)
CLOSING = (ULF, 0, 1)
RESULTS = 40
ORDER = (
    (RO1, 1), (RO1, 0), (BLK,), (RO1F, 1, 1), (RO1F, 0, 1), (RO1F, 1, 0), (RO1F, 0, 0), (FETCH,), (RO2, 1),
    (RO2, 0), (RO2F, 0, 0), (RO2F, 1, 1), (RO2F, 1, 0), (FAR, 0), (PLAIN, 0, 0), (RO2F, 0, 1), (FAR, 1), (ZF,),
    (PLAIN, 1, 0), (PLAIN, 0, 1), (PLAIN, 1, 1), (ZP,), (ZM, 1), (MERGED, 0, 1), (MERGED, 1, 0),
    (MERGED, 0, 0), (MERGED, 1, 1), (ZM, 0), (SEC, 0), (SEC, 1), (SECP, 1, 1), (SECP, 0, 0), (SECP, 1, 0),
    (SECP, 0, 1), (ZSEL,), (SECM, 0, 0), (SECM, 1, 0), (SECM, 1, 1), (SECM, 0, 1), (RL, 1), (RL, 0), (G, 0),
    (G, 1), (GL, 0), (RLF, 1, 1), (GL, 1), (RLF, 1, 0), (GLF, 1, 0), (GLF, 0, 0), (RLF, 0, 0), (GLF, 0, 1),
    (GLF, 1, 1), (RLF, 0, 1), (RG, 1), (GG, 0), (GGF, 0), (ZAF, 0, 0), (ZAF, 0, 1), (ZAF, 1, 1), (RG, 0),
    (GG, 1), (GGF, 1), (ZAF, 1, 0), (RGF, 1), (OW1, 0), (RGF, 0), (OW1, 1), (SH0,), (SH1,), (MMA,),
    (OW1F, 0, 0), (OW1F, 0, 1), (OW1F, 1, 0), (OW1F, 1, 1), (MMB,), (SP,), (SPF, 0), (SPF, 1), (OW2, 1),
    (OW2, 0), (UL, 0), (OW2F, 1, 0), (UL, 1), (ULF, 0, 1), (ULF, 1, 0), (ULF, 0, 0), (OW2F, 0, 0), (ULF, 1, 1),
    (OW2F, 1, 1), (OW2F, 0, 1), (ULE,), (OWE,),
)


def step_kernel(names, *refs):
    v = dict(zip(names, refs))
    net = Net(v["send"], v["recv"])
    t, c = net.t, net.c
    owners, g, root, blocks = v["owners"], v["g"], v["root"], v["blocks"]
    every = [v["every_0"], v["every_1"]]
    net.greet()
    right, left = net.near("z", 1), net.near("z", -1)
    plane = [wrap(t + o) for o in range(4)]
    sums = ReduceScatter(net, v["parts"], v)
    workers = Workers(net)
    steps, kept = {}, {}

    def step(name):
        def keep(function):
            steps[name] = function

        return keep

    @step((FETCH,))
    def _():
        sums.fetch((2, 1, 3, 0))

    @step((BLK,))
    def _():
        @pl.loop(0, 32)
        def _(d):
            slot, block = d * 4 + t, jnp.int32(0)
            for b in range(24):
                hit = jnp.logical_or(owners[0, b] == slot, owners[1, b] == slot)
                block = jnp.where(hit, b, block)
            blocks[d] = block

    roots = PlaneExchange(
        net, lambda s, x, y: root.at[x, y, :, s], v["root_middle"], v["roots"], v["root_relay"]
    )
    parcels = v["owned_parcels"]
    owned = PlaneExchange(
        net, lambda s, x, y: parcels.at[s, x, y], v["owned_middle"], v["results"].at[pl.ds(0, 4)], v["owned_relay"]
    )

    def pack_owned(s):
        kept["g_own", s].wait()
        for way in range(2):
            kept["g_pass", s, way].wait_recv()

        @pl.loop(0, 16)
        def _(chip):
            x, y = lax.div(chip, 4), lax.rem(chip, 4)
            for core in range(2):
                block = blocks[2 * chip + core]
                parcels[s, x, y, core] = every[s][lax.div(block, 6), lax.rem(block, 6)]

        owned.first(s)

    pieces, hold = v["roots"], v["hold"]
    far_in, plain_in, merged_in = v["z_far"], v["z_plain"], v["z_merged"]
    first_k, last_k = pl.ds(0, 6), pl.ds(6, 6)

    def wanted(target, k):
        slot = owners[lax.div(k, 6), target * 6 + lax.rem(k, 6)]
        d = lax.div(slot, 4)
        return lax.rem(slot, 4), pieces[lax.div(d, 8), lax.rem(lax.div(d, 2), 4), lax.rem(d, 2)]

    def fill(o, start, arrived=None):
        @pl.loop(0, 6)
        def _(n):
            where, rows = wanted(plane[o], start + n)
            if arrived is not None:
                rows = lax.select(where == t, rows, arrived[n])
            hold[o - 1, start + n] = rows

    @step((ZF,))
    def _():
        roots.finish()
        fill(2, 0)
        fill(2, 6)
        kept["z", 0] = [
            net.start(hold.at[1, first_k], far_in.at[0], right),
            net.start(hold.at[1, last_k], far_in.at[1], left),
        ]

    @step((ZP,))
    def _():
        fill(1, 6)
        fill(3, 0)
        kept["z", 1] = [
            net.start(hold.at[0, last_k], plain_in.at[0], right),
            net.start(hold.at[2, first_k], plain_in.at[1], left),
        ]

    @step((ZM, 0))
    def _():
        kept["z", 0][0].wait_recv()
        fill(1, 0, far_in.at[0])
        kept["z", 2] = net.start(hold.at[0, first_k], merged_in.at[0], right)

    @step((ZM, 1))
    def _():
        kept["z", 0][1].wait_recv()
        fill(3, 6, far_in.at[1])
        kept["z", 3] = net.start(hold.at[2, last_k], merged_in.at[1], left)

    root_send, root_mid = v["root_send"], v["root_mid"]

    @step((ZSEL,))
    def _():
        for copy in kept["z", 1] + [kept["z", 2], kept["z", 3]]:
            copy.wait_recv()
        for side in range(2):

            @pl.loop(0, 6)
            def _(block, side=side):
                where, rows = wanted(t, side * 6 + block)
                away = wrap(where - t)
                if side == 0:
                    other_rows = lax.select(away == 1, plain_in[1, block], merged_in[0, block])
                else:
                    other_rows = lax.select(away == 3, plain_in[0, block], merged_in[1, block])
                rows = lax.select(away == 0, rows, other_rows)
                for s in range(2):
                    line, rank = spot(s, block)
                    root_send[s, line, side, rank] = rows[s]

    g_send, g_mid = v["g_send"], v["g_mid"]

    def sum_up(s):
        sums.finish(s, g)
        here, there = g.at[:, s], every[s].at[t]
        kept["g", s] = [net.start(here, there, right), net.start(here, there, left)]
        kept["g_own", s] = net.local(here, there)

    def pass_along(s, way):
        kept["g", s][way].wait_recv()
        rows = every[s].at[plane[3], lo] if way == 0 else every[s].at[plane[1], hi]
        kept["g_pass", s, way] = net.start(rows, rows, right if way == 0 else left)

    def send_g(s):
        @pl.loop(0, 6)
        def _(block):
            line, rank = spot(s, block)
            g_send[s, line, 0, rank] = g[block, s]

        kept["gl", s] = WorkerLeg(net, s, g_send.at[s], g_mid.at[s], v["g_relay"].at[s])

    def send_roots(s):
        kept["rl", s] = WorkerLeg(net, s, root_send.at[s], root_mid.at[s], v["r_relay"].at[s])

    mats = v["mats"]

    def gather(name, leg, s, mid, first, count, relay):
        def land(j, h):
            if s == 0:
                return mats.at[pl.ds(first, count), half(h), j, c, 0]
            return mats.at[pl.ds(first, count), j, half(h), c, 1]

        kept[leg, s].finish()
        kept[name, s] = Gather(workers, s, lambda rank, h: mid.at[s, :, half(h), rank], land, relay.at[s])

    shares = [net.make(mats.at[m, :, :, c], mats.at[m, :, :, c], net.pair) for m in (2, 1)]
    net.open += [(copy, workers.is_worker) for copy in shares]
    mixed, result = v["mixed"], v["result"]

    def share(name, k):
        @pl.when(workers.is_worker)
        def _():
            for s in range(2):
                kept[name, s].wait_here()
            shares[k].start()

    def column_tiles(function):
        @pl.loop(0, 4)
        def _(n):
            function(pl.ds(pl.multiple_of(n * 256, 256), 256))

    @step((MMA,))
    def _():
        @pl.when(workers.is_worker)
        def _():
            shares[0].wait_recv()

            @column_tiles
            def _(cols):
                block = mats[2, :, :, :, :, :, cols].reshape(1024, 256)
                rows = mats[0, :, :, c].reshape(512, 1024)
                mixed[:, cols] = jnp.dot(rows, block, preferred_element_type=f32).astype(bf16)

    @step((MMB,))
    def _():
        @pl.when(workers.is_worker)
        def _():
            shares[1].wait_recv()

            @column_tiles
            def _(cols):
                block = mats[1, :, :, :, :, :, cols].reshape(1024, 256)
                rows = jnp.dot(mixed[...], block, preferred_element_type=f32).astype(bf16)
                result[:, :, :, :, cols] = rows.reshape(4, 4, 2, 16, 256)

    back, home = v["back"], v["home"]

    @step((SP,))
    def _():
        for s in range(2):
            kept["sp", s] = Spread(
                workers,
                s,
                lambda j, h, s=s: result.at[half(h), j, 0] if s == 0 else result.at[j, half(h), 1],
                lambda rank, h, s=s: back.at[s, rank, half(h)],
                v["u_relay"].at[s],
            )

    def go_home(s):
        kept["sp", s].finish()
        kept["ul", s] = HomeLeg(net, s, back.at[s], home.at[s], v["u_relay2"].at[s])

    @step((ULE,))
    def _():
        for s in range(2):
            kept["ul", s].finish()

            @pl.loop(0, 6)
            def _(block, s=s):
                line, rank = spot(s, block)
                v["update"][lax.div(block, 2), lax.rem(block, 2), s] = home[s, line, rank]

        kept["update"] = net.local(v["update"], v["results"].at[4, pl.ds(0, 3)])

    steps[(OWE,)] = owned.finish
    steps[(SH0,)] = functools.partial(share, "gg", 0)
    steps[(SH1,)] = functools.partial(share, "rg", 1)
    for s in range(2):
        bind = functools.partial
        steps[RO1, s] = bind(roots.first, s)
        steps[RO2, s] = bind(roots.second, s)
        steps[OW1, s] = bind(pack_owned, s)
        steps[OW2, s] = bind(owned.second, s)
        steps[FAR, s] = bind(sums.far, s)
        steps[SEC, s] = bind(sums.second, s)
        steps[G, s] = bind(sum_up, s)
        steps[GL, s] = bind(send_g, s)
        steps[RL, s] = bind(send_roots, s)
        steps[GG, s] = bind(gather, "gg", "gl", s, g_mid, 2, 1, v["g_relay2"])
        steps[RG, s] = bind(gather, "rg", "rl", s, root_mid, 0, 2, v["r_relay2"])
        steps[GGF, s] = lambda s=s: kept["gg", s].forward()
        steps[RGF, s] = lambda s=s: kept["rg", s].forward()
        steps[SPF, s] = lambda s=s: kept["sp", s].forward()
        steps[UL, s] = bind(go_home, s)
        for way in range(2):
            steps[PLAIN, way, s] = bind(sums.plain, way, s)
            steps[MERGED, way, s] = bind(sums.merged, way, s)
            steps[SECP, way, s] = bind(sums.second_plain, way, s)
            steps[SECM, way, s] = bind(sums.second_merged, way, s)
            steps[ZAF, s, way] = bind(pass_along, s, way)
            for name, trip, leg in ((RO1F, roots, 0), (RO2F, roots, 1), (OW1F, owned, 0), (OW2F, owned, 1)):
                steps[name, s, way] = (
                    lambda trip=trip, leg=leg, s=s, way=way: trip.legs[leg, s].forward(way)
                )
            for name, leg in ((GLF, "gl"), (RLF, "rl"), (ULF, "ul")):
                steps[name, s, way] = lambda leg=leg, s=s, way=way: kept[leg, s].forward(way)
    assert sorted(steps) == sorted(ORDER)
    for name in ORDER:
        if name == (MMA,):
            early = len(net.open)
        if name == CLOSING:
            net.close(early)
        steps[name]()
    kept["update"].wait()
    net.close(len(net.open))


def step(grads, owner_slots, root):
    tile = (16, root.shape[1])
    vmem = {
        "own": (2, 4, 6, 4),
        "cin": (2, 4, 6, 4),
        "first_in": (3, 2, 2, 3, 4),
        "f": (2, 4, 6),
        "second_in": (3, 2, 2, 3),
        "g": (6, 2),
        "every_0": (4, 6),
        "every_1": (4, 6),
        "root_middle": (2, 4, 4, 2),
        "root_relay": (2, 2, 2, 2, 2),
        "roots": (4, 4, 2, 2),
        "g_send": (2, 4, 1, 2),
        "g_mid": (2, 1, 4, 2),
        "g_relay2": (2, 2, 1, 2),
        "mats": (3, 4, 4, 2, 2),
        "owned_parcels": (2, 4, 4, 2),
        "owned_middle": (2, 4, 4, 2),
        "owned_relay": (2, 2, 2, 2, 2),
        "hold": (3, 12, 2),
        "z_far": (2, 6, 2),
        "z_plain": (2, 6, 2),
        "z_merged": (2, 6, 2),
        "root_send": (2, 4, 2, 2),
        "root_mid": (2, 2, 4, 2),
        "r_relay2": (2, 2, 2, 2),
        "result": (4, 4, 2),
        "back": (2, 2, 4),
        "home": (2, 4, 2),
        "update": (3, 2, 2),
        "u_relay": (2, 2, 2),
    }
    scratch = {name: pltpu.VMEM(shape + tile, bf16) for name, shape in vmem.items()}
    scratch["g_relay"] = pltpu.VMEM((2, 2, 1, 2, 16, tile[1] // 2), bf16)
    scratch["r_relay"] = pltpu.VMEM((2, 2, 2, 2, 16, tile[1] // 2), bf16)
    scratch["u_relay2"] = pltpu.VMEM((2, 2, 2, 16, tile[1] // 2), bf16)
    scratch["mixed"] = pltpu.VMEM((512, tile[1]), bf16)
    scratch["blocks"] = pltpu.SMEM((32,), jnp.int32)
    scratch["send"] = pltpu.SemaphoreType.DMA((256,))
    scratch["recv"] = pltpu.SemaphoreType.DMA((256,))
    names = ["parts", "owners", "root", "results"] + list(scratch)
    anywhere = pl.BlockSpec(memory_space=pl.ANY)
    return pl.pallas_call(
        functools.partial(step_kernel, names),
        out_shape=jax.ShapeDtypeStruct((RESULTS, 4, 2, 2) + tile, bf16),
        in_specs=[anywhere, pl.BlockSpec(memory_space=pltpu.SMEM), anywhere],
        out_specs=anywhere,
        scratch_shapes=list(scratch.values()),
        compiler_params=pltpu.CompilerParams(
            collective_id=0, has_side_effects=True, vmem_limit_bytes=58 * 2**20
        ),
    )(grads.reshape((6, 4, 4, 2, 2) + tile), owner_slots, root.reshape((4, 4, 2, 2) + tile))


def stats_kernel(owners, results, old_ref, new_ref, update_out, block, turned, stats, held, sem):
    me = lax.axis_index("dp") * 4 + lax.axis_index("tensor")
    copy = pltpu.make_async_copy

    def part(i):
        return pl.ds(pl.multiple_of(256 * i, 256), 256)

    def fetch(i):
        return copy(results.at[i], block.at[i], sem.at[i])

    def load(i):
        return copy(old_ref.at[part(i)], stats.at[part(i)], sem.at[4 + i])

    def store(i):
        return copy(stats.at[part(i)], new_ref.at[part(i)], sem.at[8 + i])

    take, give = copy(results.at[4, pl.ds(0, 3)], held, sem.at[12]), copy(held, update_out, sem.at[13])
    for i in range(4):
        fetch(i).start()
    for i in range(4):
        load(i).start()
    take.start()
    is_left, is_right = owners[0, 0] == me, owners[1, 0] == me
    for b in range(1, 24):
        is_left = jnp.logical_or(is_left, owners[0, b] == me)
        is_right = jnp.logical_or(is_right, owners[1, b] == me)
    named = jnp.logical_or(is_left, is_right)

    def rows(i):
        return block[i].reshape(256, 1024)

    @pl.loop(0, 4)
    def _(i):
        fetch(i).wait()

        @pl.when(named)
        def _():
            turned[:, part(i)] = rows(i).T

    take.wait()
    give.start()

    def blend(i, some, other):
        gram = jnp.dot(some, other, preferred_element_type=f32)
        stats[part(i), :] = decay_rate * stats[part(i), :] + (1 - decay_rate) * (gram * 1024 ** (-0.5))

    @pl.loop(0, 4)
    def _(i):
        load(i).wait()
        pl.when(is_left)(lambda: blend(i, rows(i), turned[...]))
        pl.when(is_right)(lambda: blend(i, turned[part(i), :], block[...].reshape(1024, 1024)))
        store(i).start()

    for i in range(4):
        store(i).wait()
    give.wait()


def finish_stats(owner_slots, results, old):
    anywhere = pl.BlockSpec(memory_space=pl.ANY)
    tile = results.shape[-2:]
    return pl.pallas_call(
        stats_kernel,
        out_shape=(
            jax.ShapeDtypeStruct(old.shape, f32),
            jax.ShapeDtypeStruct((3, 2, 2) + tile, bf16),
        ),
        in_specs=[pl.BlockSpec(memory_space=pltpu.SMEM), anywhere, anywhere],
        out_specs=(anywhere, anywhere),
        scratch_shapes=[
            pltpu.VMEM((4, 4, 2, 2) + tile, bf16),
            pltpu.VMEM((1024, 1024), bf16),
            pltpu.VMEM(old.shape, f32),
            pltpu.VMEM((3, 2, 2) + tile, bf16),
            pltpu.SemaphoreType.DMA((14,)),
        ],
        compiler_params=pltpu.CompilerParams(vmem_limit_bytes=40 * 2**20),
    )(owner_slots, results, old)


def body(partial_grads, owner_slots, statistics, inv_roots):
    owners = owner_slots.T
    results = step(partial_grads[0], owners, inv_roots[0, 0, 0])
    new_stats, update = finish_stats(owners, results, statistics[0, 0, 0])
    return (new_stats[None, None, None], update.reshape(6, 32, 1024))


def solution(mesh):
    return jax.shard_map(
        body,
        mesh=mesh,
        in_specs=(
            P("dp", "tensor", None, None),
            P(),
            P("dp", "tensor", None, None, None),
            P("dp", "tensor", None, None, None),
        ),
        out_specs=(P("dp", "tensor", None, None, None), P("tensor", "dp", None)),
        check_vma=False,
    )
```

```python
import functools

import jax
import jax.numpy as jnp
from jax import lax
from jax.experimental import pallas as pl
from jax.experimental.pallas import tpu as pltpu
from jax.sharding import PartitionSpec as P

decay_rate = 0.9
MESH = pl.DeviceIdType.MESH
f32 = jnp.float32
bf16 = jnp.bfloat16
lo, hi = pl.ds(0, 3), pl.ds(3, 3)


def place():
    d = lax.axis_index("dp")
    return lax.div(d, 8), lax.rem(lax.div(d, 2), 4), lax.rem(d, 2), lax.axis_index("tensor")


def wrap(v):
    return lax.rem(v + 8, 4)


def remote(src, dst, send, recv, device):
    return pltpu.make_async_remote_copy(
        src_ref=src, dst_ref=dst, send_sem=send, recv_sem=recv, device_id=device, device_id_type=MESH
    )


class Net:
    def __init__(self, send, recv):
        self.x, self.y, self.c, self.t = place()
        self.send, self.recv, self.count, self.open = send, recv, 0, []
        self.at = {"x": self.x, "y": self.y, "z": self.t}
        self.pair = ((self.x * 4 + self.y) * 2 + 1 - self.c, self.t)

    def near(self, axis, step, swap=0):
        x, y, t = [wrap(self.at[a] + step) if a == axis else self.at[a] for a in "xyz"]
        return ((x * 4 + y) * 2 + (1 - self.c if swap else self.c), t)

    def greet(self):
        barrier = pltpu.get_barrier_semaphore()
        peers = [self.pair] + [self.near(axis, step) for axis in "xyz" for step in (1, -1)]
        peers += [self.near(axis, step, 1) for axis in "xy" for step in (1, -1)]
        peers += [self.near(axis, 2) for axis in "xy"]
        for peer in peers:
            pl.semaphore_signal(barrier, inc=1, device_id=peer, device_id_type=MESH)
        pl.semaphore_wait(barrier, len(peers))

    def make(self, src, dst, device):
        copy = remote(src, dst, self.send.at[self.count], self.recv.at[self.count], device)
        self.count += 1
        return copy

    def start(self, src, dst, device, when=None):
        copy = self.make(src, dst, device)
        if when is None:
            copy.start()
        else:
            pl.when(when)(copy.start)
        self.open.append((copy, when))
        return copy

    def local(self, src, dst):
        copy = pltpu.make_async_copy(src, dst, self.send.at[self.count])
        self.count += 1
        copy.start()
        return copy

    def close(self, count):
        for copy, when in self.open[:count]:
            if when is None:
                copy.wait_send()
            else:
                pl.when(when)(copy.wait_send)
        self.open = self.open[count:]


ROUND = ((2, 2), (1, 1), (3, -1))


class Exchange:
    def __init__(self, net, axis, src, dst, relay):
        self.net, self.axis, self.dst, self.relay = net, axis, dst, relay
        here = net.at[axis]
        self.i = [wrap(here + o) for o in range(4)]
        right, left = net.near(axis, 1), net.near(axis, -1)
        self.far = [
            net.start(src(self.i[2], 0), relay.at[0], right),
            net.start(src(self.i[2], 1), relay.at[1], left),
        ]
        self.own = net.local(src(self.i[0], None), dst(self.i[0], None))
        self.direct = [
            net.start(src(self.i[1], None), dst(self.i[0], None), right),
            net.start(src(self.i[3], None), dst(self.i[0], None), left),
        ]

        self.passed = []

    def forward(self, way):
        self.far[way].wait_recv()
        source = self.i[3 if way == 0 else 1]
        self.passed.append(
            self.net.start(self.relay.at[way], self.dst(source, way), self.net.near(self.axis, 1 - 2 * way))
        )

    def finish(self):
        self.own.wait()
        for copy in self.direct + self.passed:
            copy.wait_recv()


def half(h):
    return slice(None) if h is None else pl.ds(2 * h, 2)


class LastLeg:
    def __init__(self, net, axis, src, dst, relay):
        self.net, self.axis, self.dst, self.relay = net, axis, dst, relay
        here = net.at[axis]
        self.i = [wrap(here + o) for o in range(4)]
        self.cores = [net.c, 1 - net.c]
        every = slice(None)
        self.far = [
            net.start(src(self.i[2], way, every), relay.at[way], net.near(axis, 1 - 2 * way)) for way in range(2)
        ]
        self.arrive = [
            net.start(src(self.i[o], None, self.cores[k]), dst(self.i[0], None), net.near(axis, step, k))
            for o, step in ((1, 1), (3, -1))
            for k in range(2)
        ]
        self.own = net.local(src(self.i[0], None, self.cores[0]), dst(self.i[0], None))
        self.arrive.append(net.start(src(self.i[0], None, self.cores[1]), dst(self.i[0], None), net.pair))

    def forward(self, way):
        net = self.net
        source = self.i[3 if way == 0 else 1]
        self.far[way].wait_recv()
        self.arrive += [
            net.start(
                self.relay.at[way, :, self.cores[k]], self.dst(source, way), net.near(self.axis, 1 - 2 * way, k)
            )
            for k in range(2)
        ]

    def finish(self):
        self.own.wait()
        for copy in self.arrive:
            copy.wait_recv()


class PlaneExchange:
    def __init__(self, net, parcels, middle, landing, relay):
        self.net, self.parcels, self.middle, self.landing, self.relay = net, parcels, middle, landing, relay
        self.legs = {}

    def first(self, s):
        a, d = self.parcels, self.middle

        def parcels(i, h):
            return a(0, i, half(h)) if s == 0 else a(1, half(h), i)

        self.legs[0, s] = Exchange(
            self.net, "xy"[s], parcels, lambda i, h: d.at[s, i, half(h)], self.relay.at[0, s]
        )

    def second(self, s):
        d, z, c = self.middle, self.landing, self.net.c
        self.legs[0, s].finish()

        def land(j, h):
            return z.at[half(h), j, c, 0] if s == 0 else z.at[j, half(h), c, 1]

        self.legs[1, s] = LastLeg(
            self.net, "yx"[s], lambda j, h, k: d.at[s, half(h), j, k], land, self.relay.at[1, s]
        )

    def finish(self):
        for s in range(2):
            self.legs[1, s].finish()


class WorkerLeg:
    def __init__(self, net, s, source, target, relay):
        self.net, self.s, self.axis = net, s, "xy"[s]
        here = net.at[self.axis]
        self.target, self.relay = target, relay
        self.i = i = [wrap(here + o) for o in range(4)]
        self.two = [v < 2 if s == 0 else v >= 2 for v in i]
        wide = relay.shape[-1]
        self.cols = [pl.ds(0, wide), pl.ds(wide, wide)]

        def when(o, rank):
            return self.two[o] if rank else None

        self.when = when
        self.far = [
            [
                net.start(
                    source.at[i[2], :, rank, :, self.cols[way]],
                    relay.at[way, :, rank],
                    net.near(self.axis, 1 - 2 * way),
                    when(2, rank),
                )
                for way in range(2)
            ]
            for rank in range(2)
        ]
        self.direct = [
            [
                net.start(
                    source.at[i[o], :, rank], target.at[:, i[0], rank], net.near(self.axis, step), when(o, rank)
                )
                for o, step in ((1, 1), (3, -1))
            ]
            for rank in range(2)
        ]
        self.own = net.local(source.at[i[0]], target.at[:, i[0]])
        self.passed = [[], []]

    def forward(self, way):
        o, goal = ((3, 1), (1, 3))[way]
        for rank in range(2):
            arrived = self.far[rank][way]
            when = self.when(goal, rank)
            if when is None:
                arrived.wait_recv()
            else:
                pl.when(when)(arrived.wait_recv)
            self.passed[rank].append(
                self.net.start(
                    self.relay.at[way, :, rank],
                    self.target.at[:, self.i[o], rank, :, self.cols[way]],
                    self.net.near(self.axis, 1 - 2 * way),
                    when,
                )
            )

    def finish(self):
        self.own.wait()
        for copy in self.direct[0] + self.passed[0]:
            copy.wait_recv()

        @pl.when(self.two[0])
        def _():
            for copy in self.direct[1] + self.passed[1]:
                copy.wait_recv()


class HomeLeg:
    def __init__(self, net, s, back, home):
        axis = "xy"[s]
        i = [wrap(net.at[axis] + o) for o in range(4)]
        self.two = [v < 2 if s == 0 else v >= 2 for v in i]
        self.arrive = [
            [
                net.start(
                    back.at[rank, i[o]], home.at[i[0], rank], net.near(axis, step), self.two[0] if rank else None
                )
                for o, step in ROUND
            ]
            for rank in range(2)
        ]
        self.own = net.local(back.at[:, i[0]], home.at[i[0]])

    def finish(self):
        self.own.wait()
        for copy in self.arrive[0]:
            copy.wait_recv()
        for copy, source in zip(self.arrive[1], (2, 3, 1)):
            pl.when(self.two[source])(copy.wait_recv)


def spot(s, block):
    rank = lax.div(block, 4)
    return block - (4, 2)[s] * rank, rank


class Workers:
    def __init__(self, net):
        self.net = net
        self.is_worker = lax.rem(net.x - net.y + 4, 2) == 0
        self.is_other = lax.rem(net.x - net.y + 4, 2) == 1
        self.ij = [(net.x, net.y), (net.y, net.x)]
        self.axes = ["y", "x"]

    def rank(self, s, step):
        i, j = self.ij[s]
        return lax.div(wrap(j + step - i), 2)

    def around(self, s):
        return [self.net.near(self.axes[s], step) for _, step in ROUND]

    def beside(self, s):
        return self.net.near(self.axes[s], 1), self.net.near(self.axes[s], -1)


class Gather:
    def __init__(self, w, s, unit, land, relay):
        self.w, net = w, w.net
        right, left = w.beside(s)
        j = [wrap(w.ij[s][1] + o) for o in range(4)]
        self.far = [
            net.make(unit(w.rank(s, 2), 0), relay.at[0], right),
            net.make(unit(w.rank(s, 2), 1), relay.at[1], left),
        ]
        self.direct = [
            net.make(unit(w.rank(s, 1), None), land(j[0], None), right),
            net.make(unit(w.rank(s, 3), None), land(j[0], None), left),
        ]
        self.passed = [
            net.make(relay.at[0], land(j[3], 0), right),
            net.make(relay.at[1], land(j[1], 1), left),
        ]
        self.own = pltpu.make_async_copy(unit(w.rank(s, 0), None), land(j[0], None), net.send.at[net.count])
        net.count += 1

        @pl.when(w.is_worker)
        def _():
            for copy in self.far + [self.own]:
                copy.start()

        @pl.when(w.is_other)
        def _():
            for copy in self.direct:
                copy.start()

        net.open += [(copy, w.is_worker) for copy in self.far]
        net.open += [(copy, w.is_other) for copy in self.direct + self.passed]

    def forward(self):
        @pl.when(self.w.is_other)
        def _():
            for arrived, onward in zip(self.far, self.passed):
                arrived.wait_recv()
                onward.start()

    def wait_here(self):
        self.own.wait()
        for copy in self.direct + self.passed:
            copy.wait_recv()


class Spread:
    def __init__(self, w, s, unit, land):
        self.w, net = w, w.net
        j = [wrap(w.ij[s][1] + o) for o in range(4)]
        here = land(w.rank(s, 0))
        self.sent = [net.make(unit(j[o]), here, device) for (o, _), device in zip(ROUND, w.around(s))]
        self.own = pltpu.make_async_copy(unit(j[0]), here, net.send.at[net.count])
        net.count += 1

        @pl.when(w.is_worker)
        def _():
            for copy in self.sent + [self.own]:
                copy.start()

        net.open += [(copy, w.is_worker) for copy in self.sent]

    def finish(self):
        @pl.when(self.w.is_other)
        def _():
            for copy in self.sent[1:]:
                copy.wait_recv()

        @pl.when(self.w.is_worker)
        def _():
            self.own.wait()
            self.sent[0].wait_recv()


class ReduceScatter:
    def __init__(self, net, parts, v):
        self.net, self.parts, self.v = net, parts, v
        at = [(net.x, net.y), (net.y, net.x)]
        self.i = [[wrap(at[s][0] + o) for o in range(4)] for s in range(2)]
        self.j = [[wrap(at[s][1] + o) for o in range(4)] for s in range(2)]
        self.loads, self.swaps, self.copies = {}, {}, {}

    def fetch(self, order):
        net, own, cin = self.net, self.v["own"], self.v["cin"]

        def view(s, i, core):
            return self.parts.at[:, i, :, core, 0] if s == 0 else self.parts.at[:, :, i, core, 1]

        for o in order:
            for s in range(2):
                i = self.i[s][o]
                self.swaps[s, o] = net.start(view(s, i, 1 - net.c), cin.at[s, i], net.pair)
                self.loads[s, o] = net.local(view(s, i, net.c), own.at[s, i])

    def ship(self, stage, s, way, src, dst):
        axis = "xy"[s] if stage < 3 else "yx"[s]
        self.copies[stage, s, way] = self.net.start(src, dst, self.net.near(axis, 1 - 2 * way))

    def ready(self, s, o):
        self.loads[s, o].wait()
        self.swaps[s, o].wait_recv()

    def add(self, out, terms, blocks):
        @pl.loop(0, blocks)
        def _(b):
            for j in range(4):
                total = terms[0][b, j].astype(f32)
                for term in terms[1:]:
                    total = total + term[b, j].astype(f32)
                out[b, j] = total.astype(bf16)

    def far(self, s):
        own, cin, first_in = self.v["own"], self.v["cin"], self.v["first_in"]
        i = self.i[s][2]
        self.ready(s, 2)
        self.add(own.at[s, i], [own.at[s, i], cin.at[s, i]], 6)
        self.ship(0, s, 0, own.at[s, i, lo], first_in.at[0, s, 0])
        self.ship(0, s, 1, own.at[s, i, hi], first_in.at[0, s, 1])

    def plain(self, way, s):
        own, cin, first_in = self.v["own"], self.v["cin"], self.v["first_in"]
        o, part = ((1, hi), (3, lo))[way]
        i = self.i[s][o]
        self.ready(s, o)
        self.add(own.at[s, i, part], [own.at[s, i, part], cin.at[s, i, part]], 3)
        self.ship(1, s, way, own.at[s, i, part], first_in.at[1, s, way])

    def merged(self, way, s):
        own, cin, first_in = self.v["own"], self.v["cin"], self.v["first_in"]
        o, part = ((1, lo), (3, hi))[way]
        i = self.i[s][o]
        self.copies[0, s, way].wait_recv()
        terms = [own.at[s, i, part], cin.at[s, i, part], first_in.at[0, s, way]]
        self.add(own.at[s, i, part], terms, 3)
        self.ship(2, s, way, own.at[s, i, part], first_in.at[2, s, way])

    def first_sum(self, s, j, k, low):
        own, cin, first_in = self.v["own"], self.v["cin"], self.v["first_in"]
        i, b = self.i[s][0], 3 * low + k
        total = own[s, i, b, j].astype(f32) + cin[s, i, b, j].astype(f32)
        total = total + first_in[2, s, low, k, j].astype(f32)
        return total + first_in[1, s, 1 - low, k, j].astype(f32)

    def first_done(self, s, j):
        f = self.v["f"]

        @pl.loop(0, 3)
        def _(k):
            for low in range(2):
                f[s, j, 3 * low + k] = self.first_sum(s, j, k, low).astype(bf16)

    def second(self, s):
        f, second_in = self.v["f"], self.v["second_in"]
        self.ready(s, 0)
        for stage in (1, 2):
            for way in range(2):
                self.copies[stage, s, way].wait_recv()
        j = self.j[s][2]
        self.first_done(s, j)
        self.ship(3, s, 0, f.at[s, j, lo], second_in.at[0, s, 0])
        self.ship(3, s, 1, f.at[s, j, hi], second_in.at[0, s, 1])

    def second_plain(self, way, s):
        f, second_in = self.v["f"], self.v["second_in"]
        o, part = ((1, hi), (3, lo))[way]
        j = self.j[s][o]
        self.first_done(s, j)
        self.ship(4, s, way, f.at[s, j, part], second_in.at[1, s, way])

    def second_merged(self, way, s):
        f, second_in = self.v["f"], self.v["second_in"]
        o, part, start = ((1, lo, 0), (3, hi, 3))[way]
        j = self.j[s][o]
        self.copies[3, s, way].wait_recv()

        @pl.loop(0, 3)
        def _(k):
            total = f[s, j, start + k].astype(f32) + second_in[0, s, way, k].astype(f32)
            f[s, j, start + k] = total.astype(bf16)

        self.ship(5, s, way, f.at[s, j, part], second_in.at[2, s, way])

    def finish(self, s, out):
        second_in = self.v["second_in"]
        for stage in (4, 5):
            for way in range(2):
                self.copies[stage, s, way].wait_recv()
        j = self.j[s][0]

        @pl.loop(0, 3)
        def _(k):
            for low in range(2):
                total = self.first_sum(s, j, k, low)
                total = total + second_in[2, s, low, k].astype(f32)
                total = total + second_in[1, s, 1 - low, k].astype(f32)
                out[3 * low + k, s] = total.astype(bf16)


(
    BLK, FAR, FETCH, G, GG, GGF, GL, GLF, MERGED, MMA, MMB, OW1, OW1F, OW2, OW2F, OWE, PLAIN, RG, RGF, RL, RLF,
    RO1, RO1F, RO2, RO2F, SEC, SECM, SECP, SH0, SH1, SP, UL, ULE, ZAF, ZF, ZM, ZP, ZSEL,
) = range(38)
CLOSING = (OW2F, 0, 0)
RESULTS = 40
ORDER = (
    (RO1, 1), (RO1, 0), (BLK,), (RO1F, 1, 1), (RO1F, 0, 1), (RO1F, 1, 0), (RO1F, 0, 0), (FETCH,), (RO2, 1),
    (RO2, 0), (RO2F, 0, 0), (RO2F, 1, 1), (RO2F, 1, 0), (FAR, 0), (PLAIN, 0, 0), (RO2F, 0, 1), (FAR, 1), (ZF,),
    (PLAIN, 1, 0), (PLAIN, 0, 1), (PLAIN, 1, 1), (ZP,), (ZM, 1), (MERGED, 0, 1), (MERGED, 1, 0),
    (MERGED, 0, 0), (MERGED, 1, 1), (ZM, 0), (SEC, 0), (SEC, 1), (SECP, 1, 1), (SECP, 0, 0), (SECP, 1, 0),
    (SECP, 0, 1), (ZSEL,), (SECM, 0, 0), (SECM, 1, 0), (SECM, 1, 1), (SECM, 0, 1), (RL, 1), (RL, 0), (G, 0),
    (G, 1), (GL, 0), (RLF, 1, 1), (GL, 1), (RLF, 1, 0), (GLF, 1, 0), (GLF, 0, 0), (RLF, 0, 0), (GLF, 0, 1),
    (GLF, 1, 1), (RLF, 0, 1), (RG, 1), (GG, 0), (GGF, 0), (ZAF, 0, 0), (ZAF, 0, 1), (ZAF, 1, 1), (RG, 0),
    (GG, 1), (GGF, 1), (ZAF, 1, 0), (RGF, 1), (OW1, 0), (RGF, 0), (OW1, 1), (SH0,), (SH1,), (MMA,),
    (OW1F, 0, 0), (OW1F, 0, 1), (OW1F, 1, 0), (OW1F, 1, 1), (MMB,), (SP,), (OW2, 1),
    (OW2, 0), (UL, 0), (OW2F, 1, 0), (UL, 1), (OW2F, 0, 0),
    (OW2F, 1, 1), (OW2F, 0, 1), (ULE,), (OWE,),
)


def step_kernel(names, *refs):
    v = dict(zip(names, refs))
    net = Net(v["send"], v["recv"])
    t, c = net.t, net.c
    owners, g, root, blocks = v["owners"], v["g"], v["root"], v["blocks"]
    every = [v["every_0"], v["every_1"]]
    net.greet()
    right, left = net.near("z", 1), net.near("z", -1)
    plane = [wrap(t + o) for o in range(4)]
    sums = ReduceScatter(net, v["parts"], v)
    workers = Workers(net)
    steps, kept = {}, {}

    def step(name):
        def keep(function):
            steps[name] = function

        return keep

    @step((FETCH,))
    def _():
        sums.fetch((2, 1, 3, 0))

    @step((BLK,))
    def _():
        @pl.loop(0, 32)
        def _(d):
            slot, block = d * 4 + t, jnp.int32(0)
            for b in range(24):
                hit = jnp.logical_or(owners[0, b] == slot, owners[1, b] == slot)
                block = jnp.where(hit, b, block)
            blocks[d] = block

    roots = PlaneExchange(
        net, lambda s, x, y: root.at[x, y, :, s], v["root_middle"], v["roots"], v["root_relay"]
    )
    parcels = v["owned_parcels"]
    owned = PlaneExchange(
        net, lambda s, x, y: parcels.at[s, x, y], v["owned_middle"], v["results"].at[pl.ds(0, 4)], v["owned_relay"]
    )

    def pack_owned(s):
        kept["g_own", s].wait()
        for way in range(2):
            kept["g_pass", s, way].wait_recv()

        @pl.loop(0, 16)
        def _(chip):
            x, y = lax.div(chip, 4), lax.rem(chip, 4)
            for core in range(2):
                block = blocks[2 * chip + core]
                parcels[s, x, y, core] = every[s][lax.div(block, 6), lax.rem(block, 6)]

        owned.first(s)

    pieces, hold = v["roots"], v["hold"]
    far_in, plain_in, merged_in = v["z_far"], v["z_plain"], v["z_merged"]
    first_k, last_k = pl.ds(0, 6), pl.ds(6, 6)

    def wanted(target, k):
        slot = owners[lax.div(k, 6), target * 6 + lax.rem(k, 6)]
        d = lax.div(slot, 4)
        return lax.rem(slot, 4), pieces[lax.div(d, 8), lax.rem(lax.div(d, 2), 4), lax.rem(d, 2)]

    def fill(o, start, arrived=None):
        @pl.loop(0, 6)
        def _(n):
            where, rows = wanted(plane[o], start + n)
            if arrived is not None:
                rows = lax.select(where == t, rows, arrived[n])
            hold[o - 1, start + n] = rows

    @step((ZF,))
    def _():
        roots.finish()
        fill(2, 0)
        fill(2, 6)
        kept["z", 0] = [
            net.start(hold.at[1, first_k], far_in.at[0], right),
            net.start(hold.at[1, last_k], far_in.at[1], left),
        ]

    @step((ZP,))
    def _():
        fill(1, 6)
        fill(3, 0)
        kept["z", 1] = [
            net.start(hold.at[0, last_k], plain_in.at[0], right),
            net.start(hold.at[2, first_k], plain_in.at[1], left),
        ]

    @step((ZM, 0))
    def _():
        kept["z", 0][0].wait_recv()
        fill(1, 0, far_in.at[0])
        kept["z", 2] = net.start(hold.at[0, first_k], merged_in.at[0], right)

    @step((ZM, 1))
    def _():
        kept["z", 0][1].wait_recv()
        fill(3, 6, far_in.at[1])
        kept["z", 3] = net.start(hold.at[2, last_k], merged_in.at[1], left)

    root_send, root_mid = v["root_send"], v["root_mid"]

    @step((ZSEL,))
    def _():
        for copy in kept["z", 1] + [kept["z", 2], kept["z", 3]]:
            copy.wait_recv()
        for side in range(2):

            @pl.loop(0, 6)
            def _(block, side=side):
                where, rows = wanted(t, side * 6 + block)
                away = wrap(where - t)
                if side == 0:
                    other_rows = lax.select(away == 1, plain_in[1, block], merged_in[0, block])
                else:
                    other_rows = lax.select(away == 3, plain_in[0, block], merged_in[1, block])
                rows = lax.select(away == 0, rows, other_rows)
                for s in range(2):
                    line, rank = spot(s, block)
                    root_send[s, line, side, rank] = rows[s]

    g_send, g_mid = v["g_send"], v["g_mid"]

    def sum_up(s):
        sums.finish(s, g)
        here, there = g.at[:, s], every[s].at[t]
        kept["g", s] = [net.start(here, there, right), net.start(here, there, left)]
        kept["g_own", s] = net.local(here, there)

    def pass_along(s, way):
        kept["g", s][way].wait_recv()
        rows = every[s].at[plane[3], lo] if way == 0 else every[s].at[plane[1], hi]
        kept["g_pass", s, way] = net.start(rows, rows, right if way == 0 else left)

    def send_g(s):
        @pl.loop(0, 6)
        def _(block):
            line, rank = spot(s, block)
            g_send[s, line, 0, rank] = g[block, s]

        kept["gl", s] = WorkerLeg(net, s, g_send.at[s], g_mid.at[s], v["g_relay"].at[s])

    def send_roots(s):
        kept["rl", s] = WorkerLeg(net, s, root_send.at[s], root_mid.at[s], v["r_relay"].at[s])

    mats = v["mats"]

    def gather(name, leg, s, mid, first, count, relay):
        def land(j, h):
            if s == 0:
                return mats.at[pl.ds(first, count), half(h), j, c, 0]
            return mats.at[pl.ds(first, count), j, half(h), c, 1]

        kept[leg, s].finish()
        kept[name, s] = Gather(workers, s, lambda rank, h: mid.at[s, :, half(h), rank], land, relay.at[s])

    shares = [net.make(mats.at[m, :, :, c], mats.at[m, :, :, c], net.pair) for m in (2, 1)]
    net.open += [(copy, workers.is_worker) for copy in shares]
    mixed, result = v["mixed"], v["result"]

    def share(name, k):
        @pl.when(workers.is_worker)
        def _():
            for s in range(2):
                kept[name, s].wait_here()
            shares[k].start()

    def column_tiles(function):
        @pl.loop(0, 4)
        def _(n):
            function(pl.ds(pl.multiple_of(n * 256, 256), 256))

    @step((MMA,))
    def _():
        @pl.when(workers.is_worker)
        def _():
            shares[0].wait_recv()

            @column_tiles
            def _(cols):
                block = mats[2, :, :, :, :, :, cols].reshape(1024, 256)
                rows = mats[0, :, :, c].reshape(512, 1024)
                mixed[:, cols] = jnp.dot(rows, block, preferred_element_type=f32).astype(bf16)

    @step((MMB,))
    def _():
        @pl.when(workers.is_worker)
        def _():
            shares[1].wait_recv()

            @column_tiles
            def _(cols):
                block = mats[1, :, :, :, :, :, cols].reshape(1024, 256)
                rows = jnp.dot(mixed[...], block, preferred_element_type=f32).astype(bf16)
                result[:, :, :, :, cols] = rows.reshape(4, 4, 2, 16, 256)

    back, home = v["back"], v["home"]

    @step((SP,))
    def _():
        for s in range(2):
            kept["sp", s] = Spread(
                workers,
                s,
                lambda j, s=s: result.at[:, j, 0] if s == 0 else result.at[j, :, 1],
                lambda rank, s=s: back.at[s, rank],
            )

    def go_home(s):
        kept["sp", s].finish()
        kept["ul", s] = HomeLeg(net, s, back.at[s], home.at[s])

    @step((ULE,))
    def _():
        for s in range(2):
            kept["ul", s].finish()

            @pl.loop(0, 6)
            def _(block, s=s):
                line, rank = spot(s, block)
                v["update"][lax.div(block, 2), lax.rem(block, 2), s] = home[s, line, rank]

        kept["update"] = net.local(v["update"], v["results"].at[4, pl.ds(0, 3)])

    steps[(OWE,)] = owned.finish
    steps[(SH0,)] = functools.partial(share, "gg", 0)
    steps[(SH1,)] = functools.partial(share, "rg", 1)
    for s in range(2):
        bind = functools.partial
        steps[RO1, s] = bind(roots.first, s)
        steps[RO2, s] = bind(roots.second, s)
        steps[OW1, s] = bind(pack_owned, s)
        steps[OW2, s] = bind(owned.second, s)
        steps[FAR, s] = bind(sums.far, s)
        steps[SEC, s] = bind(sums.second, s)
        steps[G, s] = bind(sum_up, s)
        steps[GL, s] = bind(send_g, s)
        steps[RL, s] = bind(send_roots, s)
        steps[GG, s] = bind(gather, "gg", "gl", s, g_mid, 2, 1, v["g_relay2"])
        steps[RG, s] = bind(gather, "rg", "rl", s, root_mid, 0, 2, v["r_relay2"])
        steps[GGF, s] = lambda s=s: kept["gg", s].forward()
        steps[RGF, s] = lambda s=s: kept["rg", s].forward()
        steps[UL, s] = bind(go_home, s)
        for way in range(2):
            steps[PLAIN, way, s] = bind(sums.plain, way, s)
            steps[MERGED, way, s] = bind(sums.merged, way, s)
            steps[SECP, way, s] = bind(sums.second_plain, way, s)
            steps[SECM, way, s] = bind(sums.second_merged, way, s)
            steps[ZAF, s, way] = bind(pass_along, s, way)
            for name, trip, leg in ((RO1F, roots, 0), (RO2F, roots, 1), (OW1F, owned, 0), (OW2F, owned, 1)):
                steps[name, s, way] = (
                    lambda trip=trip, leg=leg, s=s, way=way: trip.legs[leg, s].forward(way)
                )
            for name, leg in ((GLF, "gl"), (RLF, "rl")):
                steps[name, s, way] = lambda leg=leg, s=s, way=way: kept[leg, s].forward(way)
    assert sorted(steps) == sorted(ORDER)
    for name in ORDER:
        if name == (MMA,):
            early = len(net.open)
        if name == CLOSING:
            net.close(early)
        steps[name]()
    kept["update"].wait()
    net.close(len(net.open))


def step(grads, owner_slots, root):
    tile = (16, root.shape[1])
    vmem = {
        "own": (2, 4, 6, 4),
        "cin": (2, 4, 6, 4),
        "first_in": (3, 2, 2, 3, 4),
        "f": (2, 4, 6),
        "second_in": (3, 2, 2, 3),
        "g": (6, 2),
        "every_0": (4, 6),
        "every_1": (4, 6),
        "root_middle": (2, 4, 4, 2),
        "root_relay": (2, 2, 2, 2, 2),
        "roots": (4, 4, 2, 2),
        "g_send": (2, 4, 1, 2),
        "g_mid": (2, 1, 4, 2),
        "g_relay2": (2, 2, 1, 2),
        "mats": (3, 4, 4, 2, 2),
        "owned_parcels": (2, 4, 4, 2),
        "owned_middle": (2, 4, 4, 2),
        "owned_relay": (2, 2, 2, 2, 2),
        "hold": (3, 12, 2),
        "z_far": (2, 6, 2),
        "z_plain": (2, 6, 2),
        "z_merged": (2, 6, 2),
        "root_send": (2, 4, 2, 2),
        "root_mid": (2, 2, 4, 2),
        "r_relay2": (2, 2, 2, 2),
        "result": (4, 4, 2),
        "back": (2, 2, 4),
        "home": (2, 4, 2),
        "update": (3, 2, 2),
    }
    scratch = {name: pltpu.VMEM(shape + tile, bf16) for name, shape in vmem.items()}
    scratch["g_relay"] = pltpu.VMEM((2, 2, 1, 2, 16, tile[1] // 2), bf16)
    scratch["r_relay"] = pltpu.VMEM((2, 2, 2, 2, 16, tile[1] // 2), bf16)
    scratch["mixed"] = pltpu.VMEM((512, tile[1]), bf16)
    scratch["blocks"] = pltpu.SMEM((32,), jnp.int32)
    scratch["send"] = pltpu.SemaphoreType.DMA((256,))
    scratch["recv"] = pltpu.SemaphoreType.DMA((256,))
    names = ["parts", "owners", "root", "results"] + list(scratch)
    anywhere = pl.BlockSpec(memory_space=pl.ANY)
    return pl.pallas_call(
        functools.partial(step_kernel, names),
        out_shape=jax.ShapeDtypeStruct((RESULTS, 4, 2, 2) + tile, bf16),
        in_specs=[anywhere, pl.BlockSpec(memory_space=pltpu.SMEM), anywhere],
        out_specs=anywhere,
        scratch_shapes=list(scratch.values()),
        compiler_params=pltpu.CompilerParams(
            collective_id=0, has_side_effects=True, vmem_limit_bytes=58 * 2**20
        ),
    )(grads.reshape((6, 4, 4, 2, 2) + tile), owner_slots, root.reshape((4, 4, 2, 2) + tile))


def stats_kernel(owners, results, old_ref, new_ref, update_out, block, turned, stats, held, sem):
    me = lax.axis_index("dp") * 4 + lax.axis_index("tensor")
    copy = pltpu.make_async_copy

    def part(i):
        return pl.ds(pl.multiple_of(256 * i, 256), 256)

    def fetch(i):
        return copy(results.at[i], block.at[i], sem.at[i])

    load = copy(old_ref, stats, sem.at[4])

    def store(i):
        return copy(stats.at[:, part(i)], new_ref.at[:, part(i)], sem.at[8 + i])

    take, give = copy(results.at[4, pl.ds(0, 3)], held, sem.at[12]), copy(held, update_out, sem.at[13])
    for i in range(4):
        fetch(i).start()
    load.start()
    take.start()
    is_left, is_right = owners[0, 0] == me, owners[1, 0] == me
    for b in range(1, 24):
        is_left = jnp.logical_or(is_left, owners[0, b] == me)
        is_right = jnp.logical_or(is_right, owners[1, b] == me)
    named = jnp.logical_or(is_left, is_right)

    def rows(i):
        return block[i].reshape(256, 1024)

    @pl.loop(0, 4)
    def _(i):
        fetch(i).wait()

        @pl.when(named)
        def _():
            turned[:, part(i)] = rows(i).T

    take.wait()
    give.start()

    def blend(i, some, other):
        gram = jnp.dot(some, other, preferred_element_type=f32)
        stats[:, part(i)] = decay_rate * stats[:, part(i)] + (1 - decay_rate) * (gram * 1024 ** (-0.5))

    load.wait()

    @pl.loop(0, 4)
    def _(i):
        pl.when(is_left)(lambda: blend(i, block[...].reshape(1024, 1024), turned[:, part(i)]))
        pl.when(is_right)(lambda: blend(i, turned[...], block[:, :, :, :, :, part(i)].reshape(1024, 256)))
        store(i).start()

    for i in range(4):
        store(i).wait()
    give.wait()


def finish_stats(owner_slots, results, old):
    anywhere = pl.BlockSpec(memory_space=pl.ANY)
    tile = results.shape[-2:]
    return pl.pallas_call(
        stats_kernel,
        out_shape=(
            jax.ShapeDtypeStruct(old.shape, f32),
            jax.ShapeDtypeStruct((3, 2, 2) + tile, bf16),
        ),
        in_specs=[pl.BlockSpec(memory_space=pltpu.SMEM), anywhere, anywhere],
        out_specs=(anywhere, anywhere),
        scratch_shapes=[
            pltpu.VMEM((4, 4, 2, 2) + tile, bf16),
            pltpu.VMEM((1024, 1024), bf16),
            pltpu.VMEM(old.shape, f32),
            pltpu.VMEM((3, 2, 2) + tile, bf16),
            pltpu.SemaphoreType.DMA((14,)),
        ],
        compiler_params=pltpu.CompilerParams(vmem_limit_bytes=40 * 2**20),
    )(owner_slots, results, old)


def body(partial_grads, owner_slots, statistics, inv_roots):
    owners = owner_slots.T
    results = step(partial_grads[0], owners, inv_roots[0, 0, 0])
    new_stats, update = finish_stats(owners, results, statistics[0, 0, 0])
    return (new_stats[None, None, None], update.reshape(6, 32, 1024))


def solution(mesh):
    return jax.shard_map(
        body,
        mesh=mesh,
        in_specs=(
            P("dp", "tensor", None, None),
            P(),
            P("dp", "tensor", None, None, None),
            P("dp", "tensor", None, None, None),
        ),
        out_specs=(P("dp", "tensor", None, None, None), P("tensor", "dp", None)),
        check_vma=False,
    )
```
